32 devices in a mesh: dp: 8 (over z, x), tensor: 4 (over y, core).
Axes of the slice: x: 2, y: 2, z: 4, core: 2. Of those that a mesh axis runs over, the one named last changes fastest.
Arguments:
- tokens: bfloat16 [4096, 2304], P(('dp', 'tensor')), may hold values from -6 to 6
- cotangent: bfloat16 [4096, 2304], P(('dp', 'tensor')), may hold values from -6 to 6
- dealt_lengths: int32 [8, 4], P('dp'), may hold values from 0 to 512, as said below
- norm_gains: float32 [4, 2304], replicated, may hold values from 0.25 to 1.75
- query_weight: bfloat16 [2304, 2048], P('dp', 'tensor'), may hold values from -0.25 to 0.25
- key_matrix: bfloat16 [2304, 1024], P('dp', 'tensor'), may hold values from -0.125 to 0.125
- value_matrix: bfloat16 [2304, 1024], P('dp', 'tensor'), may hold values from -0.125 to 0.125
- out_weight: bfloat16 [2304, 2048], P('dp', 'tensor'), may hold values from -0.125 to 0.125
- gate_weight: bfloat16 [2304, 9216], P('dp', 'tensor'), may hold values from -0.125 to 0.125
- up_weight: bfloat16 [2304, 9216], P('dp', 'tensor'), may hold values from -0.125 to 0.125
- down_weight: bfloat16 [2304, 9216], P('dp', 'tensor'), may hold values from -0.0625 to 0.0625
- moment_query: float32 [2304, 2048], P('dp', 'tensor'), may hold values from -256 to 256
- moment_key: float32 [2304, 1024], P('dp', 'tensor'), may hold values from -256 to 256
- moment_value: float32 [2304, 1024], P('dp', 'tensor'), may hold values from -768 to 768
- moment_out: float32 [2304, 2048], P('dp', 'tensor'), may hold values from -768 to 768
- moment_gate: float32 [2304, 9216], P('dp', 'tensor'), may hold values from -768 to 768
- moment_up: float32 [2304, 9216], P('dp', 'tensor'), may hold values from -768 to 768
- moment_down: float32 [2304, 9216], P('dp', 'tensor'), may hold values from -768 to 768
Outputs:
- block_output: bfloat16 [4096, 2304], P(('dp', 'tensor'))
- input_grad: float32 [4096, 2304], P(('dp', 'tensor'))
- gain_grads: float32 [4, 2304], replicated
- grad_query: float32 [2304, 2048], P('dp', 'tensor')
- grad_key: float32 [2304, 1024], P('dp', 'tensor')
- grad_value: float32 [2304, 1024], P('dp', 'tensor')
- grad_out: float32 [2304, 2048], P('dp', 'tensor')
- grad_gate: float32 [2304, 9216], P('dp', 'tensor')
- grad_up: float32 [2304, 9216], P('dp', 'tensor')
- grad_down: float32 [2304, 9216], P('dp', 'tensor')
- momentum_query: float32 [2304, 2048], P('dp', 'tensor')
- momentum_key: float32 [2304, 1024], P('dp', 'tensor')
- momentum_value: float32 [2304, 1024], P('dp', 'tensor')
- momentum_out: float32 [2304, 2048], P('dp', 'tensor')
- momentum_gate: float32 [2304, 9216], P('dp', 'tensor')
- momentum_up: float32 [2304, 9216], P('dp', 'tensor')
- momentum_down: float32 [2304, 9216], P('dp', 'tensor')
- update_query: float32 [2304, 2048], P('dp', 'tensor')
- update_key: float32 [2304, 1024], P('dp', 'tensor')
- update_value: float32 [2304, 1024], P('dp', 'tensor')
- update_out: float32 [2304, 2048], P('dp', 'tensor')
- update_gate: float32 [2304, 9216], P('dp', 'tensor')
- update_up: float32 [2304, 9216], P('dp', 'tensor')
- update_down: float32 [2304, 9216], P('dp', 'tensor')
The draws below stay inside these ranges and needn't reach their ends.
Inputs may be any that keep to these rules, and one draw needn't show every extreme that they name: `dealt_lengths`: row g lists the lengths of the sequences dealt to group g in order, 0 only after its last sequence; padded to whole blocks of 128 slots, one row's sequences take at most 4 blocks; in every draw some row holds a single sequence of 512 tokens.
All inputs are finite; a program needn't handle non-finite values.
Results may differ from the reference program's by a relative error of at most 0.03.
Values may be sent and summed in bfloat16 or wider, within the bound.
No kernel may reach another device: no remote copies, remote signals or barrier semaphores. Data moves between devices by JAX's collectives and lax.ppermute only.
A program may use at most 384 MiB of HBM per device.

```python
import jax
import jax.numpy as jnp
from jax import lax

MODEL_WIDTH = 2304
QUERY_HEADS = 8
KEY_VALUE_HEADS = 4
HEAD_SIZE = 256
FF = 9216
WINDOW = 4096
BLK = 128
NS_STEPS = 5
GROUP_BLOCKS = 4
GROUP_SLOTS = 512
GROUPS = 8
TOKENS = 4096


def draw_dealt_lengths(key, part):
    used_key, full_key, cut_key, trim_key = jax.random.split(key, 4)
    block_index = jnp.arange(GROUP_BLOCKS, dtype=jnp.int32)
    used_blocks = jax.random.randint(used_key, (GROUPS, 1), (GROUP_BLOCKS + 1) // 2, GROUP_BLOCKS + 1, dtype=jnp.int32)
    cut_flags = jax.random.randint(cut_key, (GROUPS, GROUP_BLOCKS), 0, 2, dtype=jnp.int32)
    in_use = block_index[None, :] < used_blocks
    starts = ((block_index[None, :] == 0) | (cut_flags == 1)) & in_use
    sequence_of = jnp.cumsum(starts.astype(jnp.int32), axis=1, dtype=jnp.int32) - 1
    member = (sequence_of[:, :, None] == block_index[None, None, :]) & in_use[:, :, None]
    block_total = jnp.sum(member.astype(jnp.int32), axis=1, dtype=jnp.int32)
    trim_amount = jax.random.randint(trim_key, (GROUPS, GROUP_BLOCKS), 0, BLK, dtype=jnp.int32)
    lengths = jnp.where(block_total > 0, block_total * BLK - trim_amount, 0)
    full_group = jax.random.randint(full_key, (), 0, GROUPS, dtype=jnp.int32)
    single = jnp.where(block_index == 0, GROUP_BLOCKS * BLK, 0)
    group_index = jnp.arange(GROUPS, dtype=jnp.int32)
    lengths = jnp.where(group_index[:, None] == full_group, single[None, :], lengths)
    return lengths.astype(jnp.int32)


def draw_query_weight(key, part):
    base_key, head_key = jax.random.split(jax.random.fold_in(key, 11))
    base = jnp.clip(jax.random.normal(base_key, (MODEL_WIDTH, QUERY_HEADS, HEAD_SIZE), jnp.float32), -4.0, 4.0) * MODEL_WIDTH ** (-0.5)
    head_scale = jnp.exp(jax.random.uniform(head_key, (QUERY_HEADS,), jnp.float32, 0.7885, 1.0986))
    return (base * head_scale[None, :, None]).reshape(MODEL_WIDTH, QUERY_HEADS * HEAD_SIZE).astype(jnp.bfloat16)


def momentum_template(key, salt, columns, spread):
    own_key = jax.random.fold_in(key, salt)
    base = jnp.clip(jax.random.normal(own_key, (MODEL_WIDTH, columns), jnp.float32), -4.0, 4.0)
    return base * (spread * TOKENS ** 0.5)


def draw_moment_query(key, part):
    return momentum_template(key, 101, QUERY_HEADS * HEAD_SIZE, 0.1)


def draw_moment_key(key, part):
    return momentum_template(key, 102, KEY_VALUE_HEADS * HEAD_SIZE, 0.1)


def draw_moment_value(key, part):
    return momentum_template(key, 103, KEY_VALUE_HEADS * HEAD_SIZE, 0.3)


def draw_moment_out(key, part):
    return momentum_template(key, 104, QUERY_HEADS * HEAD_SIZE, 0.3)


def draw_moment_gate(key, part):
    return momentum_template(key, 105, FF, 0.3)


def draw_moment_up(key, part):
    return momentum_template(key, 106, FF, 0.3)


def draw_moment_down(key, part):
    return momentum_template(key, 107, FF, 0.3)


def shard_levels(stream_key, dims, pieces, low, top_value):
    level = 1.0
    for dim, blocks in pieces:
        steps = jax.random.uniform(jax.random.fold_in(jax.random.fold_in(stream_key, 6), dim), (blocks,), jnp.float32, low / len(pieces), top_value / len(pieces))
        level = level * jnp.repeat(jnp.exp(steps), dims[dim] // blocks).reshape((-1,) + (1,) * (len(dims) - 1 - dim))
    return level


def normal_values(rng, shape, width, limit, shards=(), held_as=jnp.bfloat16):
    values = jax.random.normal(rng, shape, jnp.float32) * width
    if len(shards) > 0:
        values = shard_levels(rng, shape, shards, -0.22, 0.18) * values
    return jnp.clip(values, min=-limit, max=limit).astype(held_as)


def setup_inputs(seed: int = 0) -> dict:
    seeds = jax.random.split(jax.random.key(seed), 19)
    return {
        "tokens": normal_values(seeds[0], (TOKENS, MODEL_WIDTH), 1.0, 6.0, ((0, 32),)),
        "cotangent": normal_values(seeds[1], (TOKENS, MODEL_WIDTH), 1.0, 6.0, ((0, 32),)),
        "dealt_lengths": draw_dealt_lengths(jax.random.fold_in(seeds[18], 71), 0),
        "norm_gains": jnp.clip(1.0 + 0.15 * jax.random.normal(seeds[3], (4, MODEL_WIDTH), jnp.float32), 0.25, 1.75),
        "query_weight": draw_query_weight(jax.random.fold_in(seeds[18], 71), 0),
        "key_matrix": normal_values(seeds[5], (MODEL_WIDTH, KEY_VALUE_HEADS * HEAD_SIZE), MODEL_WIDTH ** -0.5, 0.125, ((0, 8), (1, 4))),
        "value_matrix": normal_values(seeds[6], (MODEL_WIDTH, KEY_VALUE_HEADS * HEAD_SIZE), MODEL_WIDTH ** -0.5, 0.125, ((0, 8), (1, 4))),
        "out_weight": normal_values(seeds[7], (MODEL_WIDTH, QUERY_HEADS * HEAD_SIZE), (QUERY_HEADS * HEAD_SIZE) ** -0.5, 0.125, ((0, 8), (1, 4))),
        "gate_weight": normal_values(seeds[8], (MODEL_WIDTH, FF), MODEL_WIDTH ** -0.5, 0.125, ((0, 8), (1, 4))),
        "up_weight": normal_values(seeds[9], (MODEL_WIDTH, FF), MODEL_WIDTH ** -0.5, 0.125, ((0, 8), (1, 4))),
        "down_weight": normal_values(seeds[10], (MODEL_WIDTH, FF), FF ** -0.5, 0.0625, ((0, 8), (1, 4))),
        "moment_query": draw_moment_query(jax.random.fold_in(seeds[18], 71), 0),
        "moment_key": draw_moment_key(jax.random.fold_in(seeds[18], 71), 0),
        "moment_value": draw_moment_value(jax.random.fold_in(seeds[18], 71), 0),
        "moment_out": draw_moment_out(jax.random.fold_in(seeds[18], 71), 0),
        "moment_gate": draw_moment_gate(jax.random.fold_in(seeds[18], 71), 0),
        "moment_up": draw_moment_up(jax.random.fold_in(seeds[18], 71), 0),
        "moment_down": draw_moment_down(jax.random.fold_in(seeds[18], 71), 0),
    }


@jax.custom_vjp
def low(v):
    return lax.optimization_barrier(v.astype(jnp.bfloat16)).astype(jnp.float32)

@jax.custom_vjp
def low_back(v):
    return v

def low_keep(v):
    return (low(v), None)

def low_pass(kept, grad):
    return (grad,)

def back_keep(v):
    return (v, None)

def back_low(kept, grad):
    return (low(grad),)
low.defvjp(low_keep, low_pass)
low_back.defvjp(back_keep, back_low)
epsilon = 1e-06
softcap = 50.0
rope_base = 10000.0
coef_first = 3.4445
coef_second = -4.775
coef_third = 2.0315
momentum_decay = 0.95
learn_rate = 0.2
masked_value = -1e+30

def matrix_product(left_side, right_side):
    return jnp.dot(left_side, right_side, precision=lax.Precision.HIGHEST, preferred_element_type=jnp.float32)

def slot_layout(lengths):
    blocks = (lengths + BLK - 1) // BLK
    block_ends = jnp.cumsum(blocks, dtype=jnp.int32) * BLK
    slot_index = jnp.arange(GROUP_SLOTS, dtype=jnp.int32)
    passed = slot_index[:, None] >= block_ends[None, :]
    segment = lax.optimization_barrier(jnp.sum(passed.astype(jnp.int32), axis=1, dtype=jnp.int32))
    before = lax.optimization_barrier(jnp.sum(jnp.where(passed, blocks[None, :] * BLK, 0), axis=1, dtype=jnp.int32))
    position = slot_index - before
    in_segment = segment[:, None] == jnp.arange(GROUP_BLOCKS, dtype=jnp.int32)[None, :]
    own_length = lax.optimization_barrier(jnp.sum(jnp.where(in_segment, lengths[None, :], 0), axis=1, dtype=jnp.int32))
    is_alive = position < own_length
    return (segment, position, is_alive)

def allowed_pairs(segment, is_alive):
    slot_index = jnp.arange(GROUP_SLOTS, dtype=jnp.int32)
    distance = slot_index[:, None] - slot_index[None, :]
    same_segment = segment[:, None] == segment[None, :]
    inside = is_alive[:, None] & is_alive[None, :] & same_segment & (distance >= 0) & (distance < WINDOW)
    return (distance == 0) | inside

def rope_tables(position):
    half_width = HEAD_SIZE // 2
    frequency = rope_base ** (-2.0 * jnp.arange(half_width, dtype=jnp.float32) / HEAD_SIZE)
    angles = position.astype(jnp.float32)[:, None] * frequency[None, :]
    return (jnp.cos(angles), jnp.sin(angles))

def apply_rotary(values, rotary_cosines, rotary_sines):
    half_width = HEAD_SIZE // 2
    first_half = values[..., :half_width]
    second_half = values[..., half_width:]
    rotary_cosines = rotary_cosines[:, None, :]
    rotary_sines = rotary_sines[:, None, :]
    return jnp.concatenate([first_half * rotary_cosines - second_half * rotary_sines, second_half * rotary_cosines + first_half * rotary_sines], axis=-1)

def norm_scale(values, gain):
    return values * lax.rsqrt(lax.optimization_barrier(jnp.mean(values * values, axis=-1, keepdims=True)) + epsilon) * gain

def group_layer(inputs, segment, position, is_alive, weight_set, gain_set):
    query_weight, key_matrix, value_matrix, out_weight, gate_weight, up_weight, down_weight = weight_set
    rotary_cosines, rotary_sines = rope_tables(position)
    normalized_input = low(norm_scale(inputs, gain_set[0]))
    projected_queries = low_back(matrix_product(normalized_input, query_weight)).reshape(GROUP_SLOTS, QUERY_HEADS, HEAD_SIZE)
    projected_keys = low_back(matrix_product(normalized_input, key_matrix)).reshape(GROUP_SLOTS, KEY_VALUE_HEADS, HEAD_SIZE)
    value_rows_packed = low(low_back(matrix_product(normalized_input, value_matrix))).reshape(GROUP_SLOTS, KEY_VALUE_HEADS, HEAD_SIZE)
    query_rows_rotated = low(apply_rotary(projected_queries, rotary_cosines, rotary_sines) * HEAD_SIZE ** (-0.5)).reshape(GROUP_SLOTS, KEY_VALUE_HEADS, QUERY_HEADS // KEY_VALUE_HEADS, HEAD_SIZE)
    key_vectors = low(apply_rotary(projected_keys, rotary_cosines, rotary_sines))
    raw_scores = low_back(jnp.einsum('tkgd,skd->kgts', query_rows_rotated, key_vectors, precision=lax.Precision.HIGHEST))
    capped = softcap * jnp.tanh(raw_scores / softcap)
    masked = jnp.where(allowed_pairs(segment, is_alive)[None, None], capped, masked_value)
    row_max = lax.optimization_barrier(jnp.max(masked, axis=-1, keepdims=True))
    exponent = jnp.exp(masked - row_max)
    prob_low = low(exponent / lax.optimization_barrier(jnp.sum(exponent, axis=-1, keepdims=True)))
    mixed_heads = jnp.einsum('kgts,skd->tkgd', prob_low, value_rows_packed, precision=lax.Precision.HIGHEST).reshape(GROUP_SLOTS, QUERY_HEADS * HEAD_SIZE)
    mixed_heads = low(low_back(mixed_heads))
    attended = low_back(matrix_product(mixed_heads, out_weight.T))
    middle = inputs + norm_scale(attended, gain_set[1])
    normed_mid = low(norm_scale(middle, gain_set[2]))
    gate_proj = low_back(matrix_product(normed_mid, gate_weight))
    up_proj = low_back(matrix_product(normed_mid, up_weight))
    hidden = low(jax.nn.gelu(gate_proj, approximate=True) * up_proj)
    feed_out = low_back(matrix_product(hidden, down_weight.T))
    return middle + norm_scale(feed_out, gain_set[3])

def orthogonalize(block):
    current = block / (jnp.sqrt(jnp.sum(block * block)) + 1e-07)
    for repeat in range(NS_STEPS):
        square = matrix_product(current.T, current)
        polynomial = coef_second * square + coef_third * matrix_product(square, square)
        current = coef_first * current + matrix_product(current, polynomial)
    return current

def muon_update(gradient, moment):
    state = momentum_decay * moment + gradient
    blocks = state.reshape(MODEL_WIDTH, -1, HEAD_SIZE).transpose(1, 0, 2)
    ortho = lax.map(orthogonalize, blocks)
    update = -learn_rate * (MODEL_WIDTH / HEAD_SIZE) ** 0.5 * ortho.transpose(1, 0, 2).reshape(MODEL_WIDTH, -1)
    return (state, update)

def reference(tokens, cotangent, dealt_lengths, norm_gains, query_weight, key_matrix, value_matrix, out_weight, gate_weight, up_weight, down_weight, moment_query, moment_key, moment_value, moment_out, moment_gate, moment_up, moment_down):
    segment, position, is_alive = jax.vmap(slot_layout)(dealt_lengths)
    weights = tuple((w.astype(jnp.float32) for w in (query_weight, key_matrix, value_matrix, out_weight, gate_weight, up_weight, down_weight)))

    def forward(inputs, weight_set, gain_set):

        def one_group(group_item):
            return group_layer(group_item[0], group_item[1], group_item[2], group_item[3], weight_set, gain_set)
        outputs = lax.map(jax.checkpoint(one_group), (inputs.reshape(GROUPS, GROUP_SLOTS, MODEL_WIDTH), segment, position, is_alive))
        return outputs.reshape(TOKENS, MODEL_WIDTH)
    result, pullback = jax.vjp(forward, tokens.astype(jnp.float32), weights, norm_gains)
    cotangent_live = jnp.where(is_alive.reshape(TOKENS)[:, None], cotangent.astype(jnp.float32), 0.0)
    input_grad, weight_grads, gain_grads = pullback(cotangent_live)
    moments = (moment_query, moment_key, moment_value, moment_out, moment_gate, moment_up, moment_down)
    states = [muon_update(g, m) for g, m in zip(weight_grads, moments)]
    return (result.astype(jnp.bfloat16), input_grad, gain_grads, weight_grads[0], weight_grads[1], weight_grads[2], weight_grads[3], weight_grads[4], weight_grads[5], weight_grads[6], states[0][0], states[1][0], states[2][0], states[3][0], states[4][0], states[5][0], states[6][0], states[0][1], states[1][1], states[2][1], states[3][1], states[4][1], states[5][1], states[6][1])
```

```python
from functools import partial

import jax
import jax.numpy as jnp
from jax import lax
from jax.experimental import pallas as pl
from jax.experimental.pallas import tpu as pltpu
from jax.sharding import Mesh
from jax.sharding import PartitionSpec as P

MODEL_WIDTH = 2304
QUERY_HEADS = 8
KEY_VALUE_HEADS = 4
HEAD_SIZE = 256
WINDOW = 4096
BLK = 128
NS_STEPS = 5
GROUP_BLOCKS = 4
GROUP_SLOTS = 512


epsilon = 1e-06
softcap = 50.0
rope_base = 10000.0
coef_first = 3.4445
coef_second = -4.775
coef_third = 2.0315
momentum_decay = 0.95
learn_rate = 0.2
masked_value = -1e30


def slot_layout(lengths):
    blocks = (lengths + BLK - 1) // BLK
    block_ends = jnp.cumsum(blocks, dtype=jnp.int32) * BLK
    slot_index = jnp.arange(GROUP_SLOTS, dtype=jnp.int32)
    passed = slot_index[:, None] >= block_ends[None, :]
    segment = jnp.sum(passed.astype(jnp.int32), axis=1, dtype=jnp.int32)
    before = jnp.sum(jnp.where(passed, blocks[None, :] * BLK, 0), axis=1, dtype=jnp.int32)
    position = slot_index - before
    in_segment = segment[:, None] == jnp.arange(GROUP_BLOCKS, dtype=jnp.int32)[None, :]
    own_length = jnp.sum(jnp.where(in_segment, lengths[None, :], 0), axis=1, dtype=jnp.int32)
    is_alive = position < own_length
    return (segment, position, is_alive)


def allowed_pairs(segment, is_alive):
    slot_index = jnp.arange(GROUP_SLOTS, dtype=jnp.int32)
    distance = slot_index[:, None] - slot_index[None, :]
    same_segment = segment[:, None] == segment[None, :]
    inside = (
        is_alive[:, None] & is_alive[None, :] & same_segment & (distance >= 0) & (distance < WINDOW)
    )
    return (distance == 0) | inside


def rope_tables(position):
    half_width = HEAD_SIZE // 2
    frequency = rope_base ** (-2.0 * jnp.arange(half_width, dtype=jnp.float32) / HEAD_SIZE)
    angles = position.astype(jnp.float32)[:, None] * frequency[None, :]
    return (jnp.cos(angles), jnp.sin(angles))


def apply_rotary(values, rotary_cosines, rotary_sines):
    half_width = HEAD_SIZE // 2
    first_half = values[..., :half_width]
    second_half = values[..., half_width:]
    rotary_cosines = rotary_cosines[:, None, :]
    rotary_sines = rotary_sines[:, None, :]
    return jnp.concatenate(
        [
            first_half * rotary_cosines - second_half * rotary_sines,
            second_half * rotary_cosines + first_half * rotary_sines,
        ],
        axis=-1,
    )


def norm_forward(values, gain):
    inverse = lax.rsqrt(jnp.mean(values * values, axis=-1, keepdims=True) + epsilon)
    return (values * inverse * gain, inverse)


def norm_backward(values, inverse, gain, upstream):
    scaled = upstream * gain
    row_inner = jnp.mean(scaled * values, axis=-1, keepdims=True)
    return (
        inverse * scaled - values * inverse**3 * row_inner,
        jnp.sum(upstream * values * inverse, axis=0),
    )


def contract_last(left_side, right_side):
    return lax.dot_general(
        left_side, right_side, (((1,), (1,)), ((), ())), preferred_element_type=jnp.float32
    )


def contract_first(left_side, right_side):
    return lax.dot_general(
        left_side, right_side, (((0,), (0,)), ((), ())), preferred_element_type=jnp.float32
    )


def attention_scores(query_rows_rotated, key_vectors, allowed):
    raw_scores = jnp.einsum(
        "tkgd,skd->kgts", query_rows_rotated, key_vectors, preferred_element_type=jnp.float32
    )
    tanh_part = jnp.tanh(raw_scores / softcap)
    masked = jnp.where(allowed[None, None], softcap * tanh_part, masked_value)
    return (tanh_part, masked)


HALF = HEAD_SIZE // 2


def two_terms(values):
    high = values.astype(jnp.bfloat16)
    low = (values - high.astype(jnp.float32)).astype(jnp.bfloat16)
    return high, low


def product(left_side, right_side):
    return jnp.dot(left_side, right_side, preferred_element_type=jnp.float32)


def product_f32(left_terms, right_terms):
    left_high, left_low = left_terms
    right_high, right_low = right_terms
    return product(left_high, right_high) + (
        product(left_high, right_low) + product(left_low, right_high)
    )


def gram_body(counts, *refs):
    out_ref = refs[-1]
    step = pl.program_id(0)
    start = 0
    for ref, count in zip(refs[:-1], counts):

        @pl.when((step >= start) & (step < start + count))
        def _(ref=ref):
            high, low = two_terms(ref[...])
            mixed = contract_first(high, low)
            gram = contract_first(high, high) + (mixed + mixed.T)
            out_ref[0, 0] = gram[:HALF, :HALF]
            out_ref[0, 1] = gram[:HALF, HALF:]
            out_ref[0, 2] = gram[HALF:, HALF:]

        start += count

    @pl.when(step >= start)
    def _():
        out_ref[...] = jnp.zeros(out_ref.shape, out_ref.dtype)


def clamped(start, count):
    return lambda step: (0, jnp.clip(step - start, 0, count - 1))


def spans(states):
    counts = [state.shape[1] // HEAD_SIZE for state in states]
    starts = [sum(counts[:i]) for i in range(len(counts))]
    return counts, starts


def grams(states, slots):
    counts, starts = spans(states)
    rows = states[0].shape[0]
    return pl.pallas_call(
        partial(gram_body, counts),
        grid=(slots,),
        in_specs=[
            pl.BlockSpec((rows, HEAD_SIZE), clamped(s, c)) for s, c in zip(starts, counts)
        ],
        out_specs=pl.BlockSpec((1, 3, HALF, HALF), lambda step: (step, 0, 0, 0)),
        out_shape=jax.ShapeDtypeStruct((slots, 3, HALF, HALF), jnp.float32),
        cost_estimate=pl.CostEstimate(
            flops=4 * sum(counts) * rows * HEAD_SIZE**2,
            bytes_accessed=sum(counts) * 4 * HEAD_SIZE * (rows + HEAD_SIZE),
            transcendentals=0,
        ),
        compiler_params=pltpu.CompilerParams(vmem_limit_bytes=40 * 1024 * 1024),
    )(*states)


def newton_body(count, *refs):
    out_ref = refs[-1]
    row = lax.broadcasted_iota(jnp.int32, (HEAD_SIZE, HEAD_SIZE), 0)
    col = lax.broadcasted_iota(jnp.int32, (HEAD_SIZE, HEAD_SIZE), 1)
    unit = (row == col).astype(jnp.float32)
    squares = []
    scales = []
    for i in range(count):
        parts = [sum(ref[i, j].astype(jnp.float32) for ref in refs[:-1]) for j in range(3)]
        gram = jnp.concatenate(
            [
                jnp.concatenate([parts[0], parts[1]], axis=1),
                jnp.concatenate([parts[1].T, parts[2]], axis=1),
            ],
            axis=0,
        )
        total = jnp.sum(jnp.sum(gram * unit, axis=1, keepdims=True), axis=0, keepdims=True)
        inverse = 1.0 / (jnp.sqrt(total) + 1e-07)
        squares.append(gram * inverse * inverse)
        scales.append(-learn_rate * (MODEL_WIDTH / HEAD_SIZE) ** 0.5 * inverse)
    totals = [None] * count
    for repeat in range(NS_STEPS):
        terms = [two_terms(square) for square in squares]
        seconds = [product_f32(t, t) for t in terms]
        steps = [
            coef_first * unit + (coef_second * square + coef_third * second)
            for square, second in zip(squares, seconds)
        ]
        step_terms = [two_terms(step) for step in steps]
        if repeat == 0:
            totals = steps
        else:
            totals = [
                product_f32(two_terms(total), s) for total, s in zip(totals, step_terms)
            ]
        if repeat < NS_STEPS - 1:
            inner = [product_f32(s, t) for s, t in zip(step_terms, terms)]
            squares = [product_f32(two_terms(v), s) for v, s in zip(inner, step_terms)]
    for i in range(count):
        result = (totals[i] * scales[i]).astype(out_ref.dtype)
        out_ref[i, 0] = result[:HALF, :HALF]
        out_ref[i, 1] = result[:HALF, HALF:]
        out_ref[i, 2] = result[HALF:, HALF:]


def newton(pieces):
    count = pieces[0].shape[0]
    return pl.pallas_call(
        partial(newton_body, count),
        out_shape=jax.ShapeDtypeStruct((count, 3, HALF, HALF), jnp.bfloat16),
        cost_estimate=pl.CostEstimate(
            flops=count * 17 * 6 * HEAD_SIZE**3, bytes_accessed=count * 2**20, transcendentals=0
        ),
        compiler_params=pltpu.CompilerParams(vmem_limit_bytes=40 * 1024 * 1024),
    )(*pieces)


def apply_body(state_ref, factor_ref, out_ref):
    upper = factor_ref[0, 1].astype(jnp.float32)
    factor = jnp.concatenate(
        [
            jnp.concatenate([factor_ref[0, 0], factor_ref[0, 1]], axis=1),
            jnp.concatenate([upper.T.astype(jnp.bfloat16), factor_ref[0, 2]], axis=1),
        ],
        axis=0,
    )
    high, low = two_terms(state_ref[...])
    out_ref[...] = product(high, factor) + product(low, factor)


def apply_factor(state, factors, start):
    rows, cols = state.shape
    return pl.pallas_call(
        apply_body,
        grid=(cols // HEAD_SIZE,),
        in_specs=[
            pl.BlockSpec((rows, HEAD_SIZE), lambda step: (0, step)),
            pl.BlockSpec((1, 3, HALF, HALF), lambda step: (step + start, 0, 0, 0)),
        ],
        out_specs=pl.BlockSpec((rows, HEAD_SIZE), lambda step: (0, step)),
        out_shape=jax.ShapeDtypeStruct((rows, cols), jnp.float32),
        cost_estimate=pl.CostEstimate(
            flops=4 * rows * cols * HEAD_SIZE, bytes_accessed=8 * rows * cols, transcendentals=0
        ),
        compiler_params=pltpu.CompilerParams(vmem_limit_bytes=40 * 1024 * 1024),
    )(state, factors)


VMEM_BYTES = 50 * 1024 * 1024


def dense_call(body, grid, in_specs, out_specs, out_shape, flops, *operands):
    outs = out_shape if isinstance(out_shape, (list, tuple)) else [out_shape]
    moved = sum(v.size * v.dtype.itemsize for v in operands) + sum(
        v.size * v.dtype.itemsize for v in outs
    )
    return pl.pallas_call(
        body,
        grid=grid,
        in_specs=in_specs,
        out_specs=out_specs,
        out_shape=out_shape,
        cost_estimate=pl.CostEstimate(flops=flops, bytes_accessed=moved, transcendentals=0),
        compiler_params=pltpu.CompilerParams(vmem_limit_bytes=VMEM_BYTES),
    )(*operands)


def column_tile(width):
    return width if width % 768 else 768


def enter_body(rows_ref, gate_ref, up_ref, hidden_ref, gelu_ref, pull_ref):
    rows = rows_ref[...]
    gate = product(rows, gate_ref[...])
    up = product(rows, up_ref[...])
    factor = (2.0 / jnp.pi) ** 0.5
    squared = gate * gate
    bend = jnp.tanh(factor * (gate + 0.044715 * gate * squared))
    upper = 0.5 * (1.0 + bend)
    gelu = gate * upper
    slope = upper + 0.5 * gate * (1.0 - bend * bend) * (factor * (1.0 + 0.134145 * squared))
    hidden_ref[...] = (gelu * up).astype(jnp.bfloat16)
    gelu_ref[...] = gelu.astype(jnp.bfloat16)
    pull_ref[...] = (up * slope).astype(jnp.bfloat16)


def enter(rows, gate, up):
    count, width = rows.shape
    pieces, _, cols = gate.shape
    tile = column_tile(cols)
    weight = pl.BlockSpec((None, width, tile), lambda p, j, i: (p, 0, j))
    out = pl.BlockSpec((None, 256, tile), lambda p, j, i: (p, i, j))
    return dense_call(
        enter_body,
        (pieces, cols // tile, count // 256),
        [pl.BlockSpec((256, width), lambda p, j, i: (i, 0)), weight, weight],
        [out] * 3,
        [jax.ShapeDtypeStruct((pieces, count, cols), jnp.bfloat16)] * 3,
        4 * count * width * cols * pieces,
        rows,
        gate,
        up,
    )


def leave_body(rows_ref, down_ref, gelu_ref, pull_ref, gate_ref, up_ref):
    delta = product(rows_ref[...], down_ref[...])
    gate_ref[...] = (delta * pull_ref[...].astype(jnp.float32)).astype(jnp.bfloat16)
    up_ref[...] = (delta * gelu_ref[...].astype(jnp.float32)).astype(jnp.bfloat16)


def leave(rows, down, gelu, pull):
    count, width = rows.shape
    pieces, _, cols = down.shape
    tile = column_tile(cols)
    out = pl.BlockSpec((None, 256, tile), lambda p, j, i: (p, i, j))
    return dense_call(
        leave_body,
        (pieces, cols // tile, count // 256),
        [
            pl.BlockSpec((256, width), lambda p, j, i: (i, 0)),
            pl.BlockSpec((None, width, tile), lambda p, j, i: (p, 0, j)),
            out,
            out,
        ],
        [out] * 2,
        [jax.ShapeDtypeStruct((pieces, count, cols), jnp.bfloat16)] * 2,
        2 * count * width * cols * pieces,
        rows,
        down,
        gelu,
        pull,
    )


def shrink_body(count, *refs):
    pieces = refs[0].shape[0]
    total = None
    for i in range(count):
        for p in range(pieces):
            term = contract_last(refs[i][p], refs[count + i][p])
            total = term if total is None else total + term
    refs[-1][...] = total.astype(refs[-1].dtype)


def shrink(lefts, rights, rows, part, dtype):
    pieces, width, cols = rights[0].shape
    count = len(lefts)
    tile = 768 if cols < 768 else 256
    return dense_call(
        partial(shrink_body, count),
        (width // tile,),
        [pl.BlockSpec((pieces, rows, cols), lambda j: (0, part, 0))] * count
        + [pl.BlockSpec((pieces, tile, cols), lambda j: (0, j, 0))] * count,
        pl.BlockSpec((rows, tile), lambda j: (0, j)),
        jax.ShapeDtypeStruct((rows, width), dtype),
        2 * rows * width * cols * pieces * count,
        *lefts,
        *rights,
    )


def outer_body(left_ref, right_ref, out_ref):
    left = left_ref[...]
    for p in range(out_ref.shape[0]):
        out_ref[p] = contract_first(left, right_ref[p]).astype(jnp.bfloat16)


def outer(left, right):
    rows, width = left.shape
    pieces, _, cols = right.shape
    tile = 384 if cols < 768 else 256
    return dense_call(
        outer_body,
        (width // tile,),
        [
            pl.BlockSpec((rows, tile), lambda j: (0, j)),
            pl.BlockSpec((pieces, rows, cols), lambda j: (0, 0, 0)),
        ],
        pl.BlockSpec((pieces, tile, cols), lambda j: (0, j, 0)),
        jax.ShapeDtypeStruct((pieces, width, cols), jnp.bfloat16),
        2 * pieces * rows * width * cols,
        left,
        right,
    )


def fence(*values):
    return lax.optimization_barrier(values)


def after(value, *others):
    return lax.optimization_barrier((value,) + others)[0]


class Plain:
    def __init__(self, sizes):
        self.owners = sizes["dp"]
        self.token_spec = P(("dp", "tensor"), None)
        self.length_spec = P("dp", None)
        self.weight_spec = P("dp", "tensor")
        self.every = ("dp", "tensor")

    def setup(self):
        self.part = lax.axis_index("tensor")

    def gather_dp(self, shard):
        return lax.all_gather(shard, "dp", axis=0, tiled=True)

    def scatter_dp(self, partial_sum):
        return wide(lax.psum_scatter(partial_sum, "dp", scatter_dimension=0, tiled=True))

    def open(self, normed, mixed, out, gate, up, down, moments):
        self.later = {"up": up, "down": down}
        return (
            self.attn_rows(normed),
            self.gather_dp(mixed),
            self.gather_dp(out),
            self.gather_dp(gate)[None],
        )

    def beside(self, values, name):
        return values, self.gather_dp(self.later[name])[None]

    def beside_hidden(self, values):
        return values

    def attn_rows(self, values):
        return lax.all_gather(values, "tensor", axis=0, tiled=True)

    def attn_sum(self, values):
        return lax.psum_scatter(values, "tensor", scatter_dimension=0, tiled=True)

    def features_in(self, values):
        return values

    def features_out(self, values):
        return values

    def mlp_sum_rows(self, partial_sums):
        return self.scatter_dp(partial_sums[0])

    def close(self, partial_out, attention_backward, totals, moments):
        partial_mixed, partial_normed = attention_backward(partial_out)[:2]
        cuts = (moments[0].shape[1], moments[0].shape[1] + moments[1].shape[1])
        grads = jnp.split(self.scatter_dp(partial_mixed), cuts, axis=1)
        grads = (*grads, self.scatter_dp(partial_out), totals[1], totals[2], totals[0])
        states = [momentum_decay * m + g for m, g in zip(moments, grads)]
        first = muon(self, states[6:] + states[4:5])
        last = muon(self, states[5:6] + states[:4])
        updates = (*last[1:], first[1], last[0], first[0])
        return grads, states, updates, self.attn_sum(partial_normed)

    def finish_gains(self, gains):
        return self.sum_every(gains)

    def sum_every(self, values):
        return lax.psum(values, self.every)

    def mlp_rows(self, values):
        return self.attn_rows(values)

    def mlp_sum(self, lefts, rights):
        values = shrink(lefts, rights, lefts[0].shape[1], 0, jnp.float32)
        return self.attn_sum(values), values

    def gram_sum(self, values):
        return [lax.psum_scatter(values, "dp", scatter_dimension=0, tiled=True)]

    def factor_gather(self, values):
        return lax.all_gather(values, "dp", axis=0, tiled=True)


def shift(values, axis, distance):
    size = lax.axis_size(axis)
    return lax.ppermute(values, axis, [(i, (i + distance) % size) for i in range(size)])


def pick(stacked, index):
    return lax.dynamic_index_in_dim(stacked, index, 0, keepdims=False)


def wide(values):
    return values.astype(jnp.float32)


def narrow(values):
    return values.astype(jnp.bfloat16)


def place(buffer, values, *index):
    fresh = values.reshape((1,) * len(index) + values.shape)
    zero = jnp.zeros((), jnp.int32)
    return lax.dynamic_update_slice(buffer, fresh, tuple(index) + (zero,) * values.ndim)


class Grid:
    def __init__(self, sizes):
        self.depth = sizes["z"]
        self.owners = sizes["z"] * sizes["x"]
        self.token_spec = P(("z", "x", "y", "c"), None)
        self.length_spec = P(("z", "x"), None)
        self.weight_spec = P(("z", "x"), ("y", "c"))
        self.every = ("z", "x", "y", "c")

    def setup(self):
        self.z, self.x, self.y, self.c = (lax.axis_index(a) for a in self.every)
        self.part = self.y * 2 + self.c


    def features_in(self, values):
        split = values.reshape(values.shape[:-1] + (self.depth, 2, -1))
        return jnp.swapaxes(split, -3, -2).reshape(values.shape)

    def features_out(self, values):
        split = values.reshape(values.shape[:-1] + (2, self.depth, -1))
        return jnp.swapaxes(split, -3, -2).reshape(values.shape)

    def back(self, distance):
        return lax.rem(self.z + self.depth - distance, self.depth)

    def ahead(self, distance):
        return lax.rem(self.z + distance, self.depth)

    def open(self, normed, mixed, out, gate, up, down, moments):
        attn = jnp.concatenate([mixed, out], axis=1)
        line = [attn, shift(attn, "z", 1)]
        across = [shift(attn, "x", 1)]
        over = shift(normed, "y", 1)
        across[0], line[1], over, gate, up = fence(across[0], line[1], over, gate, up)

        across.append(shift(line[1], "x", 1))
        line.append(shift(line[1], "z", 1))
        pair = shift(jnp.concatenate([normed, over], axis=0), "c", 1)
        gate_sent = self.send(self.quarters(gate))
        across[1], line[2], pair, up, down, *gate_sent = fence(
            across[1], line[2], pair, up, down, *gate_sent
        )

        across.append(shift(line[2], "x", 1))
        line.append(shift(line[2], "z", 1))
        up_sent = self.send(self.quarters(up))
        across[2], line[3], down, gate_sent, up_sent, moments = lax.optimization_barrier(
            (across[2], line[3], down, gate_sent, up_sent, moments)
        )

        across.append(shift(line[3], "x", 1))
        gate_arrived = self.arrive(gate_sent)
        down_sent = self.send(self.quarters(down))
        inner = [self.main_quarters(narrow(m)) for m in moments]
        inner_sent = [
            self.send(jnp.concatenate([inner[0], inner[1]], axis=2)),
            self.send(inner[2]),
        ]
        across[3], gate_arrived, up_sent, down_sent, inner_sent = lax.optimization_barrier(
            (across[3], gate_arrived, up_sent, down_sent, inner_sent)
        )
        self.sent = {"up": up_sent, "down": down_sent}
        self.inner_sent = inner_sent

        mixed_cols = mixed.shape[1]
        full = jnp.zeros((2, self.depth) + attn.shape, attn.dtype)
        for k in range(self.depth):
            full = place(full, line[k], self.x, self.back(k))
            full = place(full, across[k], 1 - self.x, self.back(k))
        full, gate_column = fence(full.reshape((-1,) + attn.shape[1:]), self.column(gate_arrived))
        return (
            self.order_rows(normed, over, pair),
            full[:, :mixed_cols],
            full[:, mixed_cols:],
            self.gather_plane(gate_column),
        )

    def beside(self, values, name):
        arrived = self.arrive(self.sent[name])
        values, arrived = lax.optimization_barrier((values, arrived))
        values, column, self.sent = lax.optimization_barrier(
            (values, self.column(arrived), self.sent)
        )
        return values, self.gather_plane(column)

    def beside_hidden(self, values):
        arrived = self.arrive(self.inner_sent[0])
        values, arrived, last = lax.optimization_barrier((values, arrived, self.inner_sent[1]))
        self.inner_sent = last
        self.inner = jnp.split(self.column(arrived), 2, axis=2)
        return values


    def main_quarters(self, shard):
        rows, cols = shard.shape
        self.main = cols // (self.depth * HEAD_SIZE) * HEAD_SIZE
        main = shard[:, : self.depth * self.main]
        return main.reshape(rows, self.depth, self.main).transpose(1, 0, 2)

    def quarters(self, shard):
        main = self.main_quarters(shard)
        rest = shard[:, self.depth * self.main :]
        rest = rest.reshape(shard.shape[0], self.depth, -1).transpose(1, 0, 2)
        return jnp.concatenate([main, rest], axis=2)

    def send(self, chunks):
        return [pick(chunks, self.ahead(k)) for k in range(self.depth)]

    def arrive(self, sent):
        return [sent[0]] + [shift(sent[k], "z", k) for k in range(1, self.depth)]

    def column(self, arrived):
        column = jnp.zeros((self.depth,) + arrived[0].shape, arrived[0].dtype)
        for k, values in enumerate(arrived):
            column = place(column, values, self.back(k))
        return column

    def gather_plane(self, column):
        full = lax.all_gather(column, ("y", "x"), axis=0, tiled=True)
        return full.reshape(2, 2 * self.depth * column.shape[1], -1)

    def order_rows(self, own, over, pair):
        rows = own.shape[0]
        near, far = pair[:rows], pair[rows:]
        first = self.y == 0
        low_own, high_own = jnp.where(first, own, over), jnp.where(first, over, own)
        low_near, high_near = jnp.where(first, near, far), jnp.where(first, far, near)
        core = self.c == 0
        return jnp.concatenate(
            [
                jnp.where(core, low_own, low_near),
                jnp.where(core, low_near, low_own),
                jnp.where(core, high_own, high_near),
                jnp.where(core, high_near, high_own),
            ],
            axis=0,
        )

    def attn_rows(self, values):
        over = shift(values, "y", 1)
        pair = shift(jnp.concatenate([values, over], axis=0), "c", 1)
        return self.order_rows(values, over, pair)

    def core_half(self, values):
        stacked = values.reshape(2, 2, -1, values.shape[1]).transpose(1, 0, 2, 3)
        return pick(stacked, self.c), narrow(pick(stacked, 1 - self.c))

    def attn_sum(self, values):
        kept, sent = self.core_half(values)
        mine = kept + wide(shift(sent, "c", 1))
        return pick(mine, self.y) + wide(shift(narrow(pick(mine, 1 - self.y)), "y", 1))

    def mlp_sum_rows(self, partial_sums):
        stacked = partial_sums.reshape(4 * self.depth, -1, partial_sums.shape[-1])
        return lax.psum_scatter(stacked, ("y", "x"), scatter_dimension=0, tiled=True)

    def mlp_finish(self, arrived):
        column = self.column(arrived)
        rows = column.shape[1]
        main = column[:, :, : self.main].transpose(1, 0, 2).reshape(rows, -1)
        rest = column[:, :, self.main :].transpose(1, 0, 2).reshape(rows, -1)
        return wide(jnp.concatenate([main, rest], axis=1))

    def mlp_rows(self, values):
        line = jnp.concatenate([shift(values, "z", k) for k in range(1, self.depth)], axis=0)
        return jnp.concatenate([values, line, shift(values, "c", 1), shift(line, "c", 1)], axis=0)

    def mlp_sum(self, lefts, rights):
        rows = lefts[0].shape[1] // 2
        away = shrink(lefts, rights, rows, 1, jnp.bfloat16)
        received = shift(away, "c", 1)
        kept = shrink([after(v, away) for v in lefts], rights, rows, 0, jnp.bfloat16)
        mine = (wide(kept) + wide(received)).reshape(self.depth, -1, kept.shape[1])
        sent = [narrow(mine[k]) for k in range(1, self.depth)]
        own, *sent = fence(mine[0], *sent)
        arrived = [shift(v, "z", self.depth - k) for k, v in enumerate(sent, 1)]
        return own + sum(wide(v) for v in arrived), own

    def halves(self, values):
        stacked = values.reshape((2, -1) + values.shape[1:])
        return pick(stacked, self.x), pick(stacked, 1 - self.x)

    def main_grams(self, total, inner):
        state = momentum_decay * wide(inner) + wide(total[:, :, : self.main])
        return self.halves(grams([state.reshape(-1, self.main)], self.main // HEAD_SIZE))

    def close(self, partial_out, attention_backward, totals, moments):
        total_down, total_gate, total_up = totals

        stacked = partial_out.reshape(2, -1, partial_out.shape[1])
        kept_out, sent_out = pick(stacked, self.x), pick(stacked, 1 - self.x)
        down_sent = self.send(total_down)
        partial_out, sent_out, down_sent = lax.optimization_barrier(
            (partial_out, sent_out, down_sent)
        )
        received = shift(sent_out, "x", 1)
        turned_down = self.arrive(down_sent)
        backward = attention_backward(partial_out)
        backward, received, turned_down, total_gate = lax.optimization_barrier(
            (backward, received, turned_down, total_gate)
        )
        partial_mixed, partial_normed = backward
        out_rows = (wide(kept_out) + wide(received)).reshape(self.depth, -1, kept_out.shape[1])
        out_sent = self.send(narrow(out_rows))
        stacked = partial_mixed.reshape(2, -1, partial_mixed.shape[1])
        kept_mixed, sent_mixed = pick(stacked, self.x), pick(stacked, 1 - self.x)
        kept_normed, sent_normed = self.core_half(partial_normed)
        out_sent, sent_mixed, sent_normed = lax.optimization_barrier(
            (out_sent, sent_mixed, sent_normed)
        )

        received = shift(sent_mixed, "x", 1)
        out_arrived = self.arrive(out_sent)
        normed_received = shift(sent_normed, "c", 1)
        grad_down = self.mlp_finish(turned_down)
        kept_grams, sent_grams = zip(
            self.main_grams(total_down, self.inner[0]), self.main_grams(total_gate, self.inner[1])
        )
        kept_grams, sent_grams = jnp.concatenate(kept_grams), jnp.concatenate(sent_grams)
        received, out_arrived, normed_received, sent_grams, total_up = lax.optimization_barrier(
            (received, out_arrived, normed_received, sent_grams, total_up)
        )

        mixed_rows = (wide(kept_mixed) + wide(received)).reshape(
            self.depth, -1, kept_mixed.shape[1]
        )
        mixed_arrived = self.arrive(self.send(narrow(mixed_rows)))
        received_grams = shift(sent_grams, "x", 1)
        mine = kept_normed + wide(normed_received)
        normed_received = shift(narrow(pick(mine, 1 - self.y)), "y", 1)
        inner_arrived = self.arrive(self.inner_sent)
        grad_out = sum(wide(v) for v in out_arrived)
        both_sent = [jnp.concatenate(v, axis=0) for v in zip(self.send(total_gate), self.send(total_up))]
        (
            mixed_arrived,
            received_grams,
            normed_received,
            both_sent,
            inner_arrived,
        ) = lax.optimization_barrier(
            (mixed_arrived, received_grams, normed_received, both_sent, inner_arrived)
        )
        summed_normed = pick(mine, self.y) + wide(normed_received)

        both_arrived = self.arrive(both_sent)
        grad_mixed = sum(wide(v) for v in mixed_arrived)
        cuts = (moments[0].shape[1], moments[0].shape[1] + moments[1].shape[1])
        grads = [*jnp.split(grad_mixed, cuts, axis=1), grad_out]
        states = [momentum_decay * m + g for m, g in zip(moments, grads)]
        kept_attn, sent_attn = self.halves(grams(states, self.owners))
        received_attn = shift(sent_attn, "x", 1)
        kept_last, sent_last = self.main_grams(total_up, self.column(inner_arrived))
        received_last = shift(sent_last, "x", 1)
        both_arrived, received_attn, received_last = lax.optimization_barrier(
            (both_arrived, received_attn, received_last)
        )

        rows = both_arrived[0].shape[0] // 2
        grad_gate = self.mlp_finish([v[:rows] for v in both_arrived])
        grad_up = self.mlp_finish([v[rows:] for v in both_arrived])
        grads += [grad_gate, grad_up, grad_down]
        states += [momentum_decay * m + g for m, g in zip(moments[4:], grads[4:])]
        attn_arrived = self.arrive(self.send((kept_attn + received_attn)[:, None]))
        kept_rest, sent_rest = self.halves(
            grams([v[:, -HEAD_SIZE:] for v in states[4:]], self.owners)
        )
        received_rest = shift(sent_rest, "x", 1)
        main_factors = newton(
            [
                jnp.concatenate([kept_grams, kept_last]),
                jnp.concatenate([received_grams, received_last]),
            ]
        )
        attn_arrived, received_rest, main_factors = lax.optimization_barrier(
            (attn_arrived, received_rest, main_factors)
        )

        rest_arrived = self.arrive(self.send((kept_rest + received_rest)[:, None]))
        factors = jnp.concatenate([main_factors, newton(attn_arrived)])
        rest_arrived, factors = lax.optimization_barrier((rest_arrived, factors))

        line = self.along(factors)
        rest_factors = newton(rest_arrived)
        line, rest_factors = fence(line, rest_factors)

        across = shift(line, "x", 1)
        rest_line = self.along(rest_factors)
        across, rest_line = fence(across, rest_line)

        rest = self.both(rest_line, shift(rest_line, "x", 1))[:, :, 0]
        rest = rest.reshape((-1,) + rest.shape[2:])
        full = self.both(line, across)
        attn_factors = full[:, :, 3].reshape((-1,) + full.shape[3:])
        main = full[:, :, :3].transpose(2, 1, 0, 3, 4, 5).reshape((3, -1) + full.shape[3:])
        counts, starts = spans(states[:4])
        updates = [apply_factor(v, attn_factors, s) for v, s in zip(states[:4], starts)]
        for i, order in enumerate((1, 2, 0)):
            updates.append(
                apply_factor(
                    states[4 + i], jnp.concatenate([main[order], rest[i : i + 1]], axis=0), 0
                )
            )
        self.last = line
        return grads, states, updates, summed_normed

    def along(self, values):
        line = jnp.zeros((self.depth,) + values.shape, values.dtype)
        for k in range(self.depth):
            line = place(line, shift(values, "z", k) if k else values, self.back(k))
        return line

    def both(self, line, across):
        full = jnp.zeros((2,) + line.shape, line.dtype)
        return place(place(full, line, self.x), across, 1 - self.x)

    def finish_gains(self, gains):
        for axis in ("c", "y", "x"):
            gains = gains + shift(gains, axis, 1)
        return gains + sum(shift(gains, "z", k) for k in range(1, self.depth))


def muon(ways, states):
    counts, starts = spans(states)
    slots = -(-sum(counts) // ways.owners) * ways.owners
    factors = ways.factor_gather(newton(ways.gram_sum(grams(states, slots))))
    return [apply_factor(state, factors, start) for state, start in zip(states, starts)]


def shards(
    ways,
    tokens,
    cotangent,
    dealt_lengths,
    norm_gains,
    query_weight,
    key_matrix,
    value_matrix,
    out_weight,
    gate_weight,
    up_weight,
    down_weight,
    moment_query,
    moment_key,
    moment_value,
    moment_out,
    moment_gate,
    moment_up,
    moment_down,
):
    ways.setup()
    local_rows = tokens.shape[0]
    segment, position, is_alive = slot_layout(dealt_lengths[0])
    allowed = allowed_pairs(segment, is_alive)
    rotary_cosines, rotary_sines = rope_tables(position)
    my_alive = lax.dynamic_slice_in_dim(is_alive, ways.part * local_rows, local_rows)
    query_cols = query_weight.shape[1]
    kv_cols = key_matrix.shape[1]
    kv_heads = kv_cols // HEAD_SIZE
    group_width = QUERY_HEADS // KEY_VALUE_HEADS
    cuts = (query_cols, query_cols + kv_cols)

    norm_gains = ways.features_in(norm_gains)
    inputs = ways.features_in(tokens).astype(jnp.float32)
    normalized_input, inverse_in = norm_forward(inputs, norm_gains[0])
    normed_full, mixed_full, out_full, gate_full = ways.open(
        normalized_input.astype(jnp.bfloat16),
        jnp.concatenate([query_weight, key_matrix, value_matrix], axis=1),
        out_weight,
        gate_weight,
        up_weight,
        down_weight,
        (moment_down, moment_gate, moment_up),
    )
    projected = jnp.dot(normed_full, mixed_full, preferred_element_type=jnp.float32)
    projected_queries, projected_keys, projected_values = jnp.split(projected, cuts, axis=1)
    projected_queries = projected_queries.reshape(GROUP_SLOTS, -1, HEAD_SIZE)
    projected_keys = projected_keys.reshape(GROUP_SLOTS, kv_heads, HEAD_SIZE)
    value_rows_packed = projected_values.astype(jnp.bfloat16).reshape(
        GROUP_SLOTS, kv_heads, HEAD_SIZE
    )
    query_rows_rotated = (
        (apply_rotary(projected_queries, rotary_cosines, rotary_sines) * HEAD_SIZE ** (-0.5))
        .astype(jnp.bfloat16)
        .reshape(GROUP_SLOTS, kv_heads, group_width, HEAD_SIZE)
    )
    key_vectors = apply_rotary(projected_keys, rotary_cosines, rotary_sines).astype(jnp.bfloat16)
    tanh_part, masked = attention_scores(query_rows_rotated, key_vectors, allowed)
    row_max = jnp.max(masked, axis=-1, keepdims=True)
    exponent = jnp.exp(masked - row_max)
    row_total = jnp.sum(exponent, axis=-1, keepdims=True)
    prob_exact = exponent / row_total
    prob_low = prob_exact.astype(jnp.bfloat16)
    mixed_heads = (
        jnp.einsum(
            "kgts,skd->tkgd", prob_low, value_rows_packed, preferred_element_type=jnp.float32
        )
        .reshape(GROUP_SLOTS, query_cols)
        .astype(jnp.bfloat16)
    )
    partial_attended, up_full = ways.beside(contract_last(mixed_heads, out_full), "up")
    attended, down_full = ways.beside(ways.attn_sum(partial_attended), "down")
    normed_attn, inverse_attn = norm_forward(attended, norm_gains[1])
    middle = inputs + normed_attn
    normed_mid, inverse_mid = norm_forward(middle, norm_gains[2])
    mid_full = ways.mlp_rows(normed_mid.astype(jnp.bfloat16))
    hidden, activated, pulled = enter(mid_full, gate_full, up_full)
    hidden = ways.beside_hidden(hidden)
    feed_out, _ = ways.mlp_sum([hidden], [down_full])
    normed_feed, inverse_feed = norm_forward(feed_out, norm_gains[3])
    block_output = (middle + normed_feed).astype(jnp.bfloat16)

    upstream = jnp.where(my_alive[:, None], ways.features_in(cotangent).astype(jnp.float32), 0.0)
    delta_feed, gain_feed = norm_backward(feed_out, inverse_feed, norm_gains[3], upstream)
    feed_grad = ways.mlp_rows(delta_feed.astype(jnp.bfloat16))
    partial_down = outer(feed_grad, hidden)
    total_down = ways.mlp_sum_rows(partial_down)
    feed_grad = after(feed_grad, partial_down)
    delta_gate, delta_up = leave(feed_grad, down_full, activated, pulled)
    delta_mid, token = ways.mlp_sum([delta_gate, delta_up], [gate_full, up_full])
    mid_again = after(mid_full, token)
    total_gate = ways.mlp_sum_rows(outer(mid_again, delta_gate))
    total_up = ways.mlp_sum_rows(outer(mid_again, delta_up))

    mid_back, gain_mid = norm_backward(middle, inverse_mid, norm_gains[2], delta_mid)
    delta_middle = upstream + mid_back
    delta_attended, gain_attn = norm_backward(attended, inverse_attn, norm_gains[1], delta_middle)
    attn_grad = ways.attn_rows(delta_attended.astype(jnp.bfloat16))
    partial_out = narrow(contract_first(attn_grad, mixed_heads))

    def attention_backward(start):
        delta_mixed = (
            jnp.dot(after(attn_grad, start), out_full, preferred_element_type=jnp.float32)
            .astype(jnp.bfloat16)
            .reshape(GROUP_SLOTS, kv_heads, group_width, HEAD_SIZE)
        )
        delta_prob = jnp.einsum(
            "tkgd,skd->kgts", delta_mixed, value_rows_packed, preferred_element_type=jnp.float32
        )
        delta_values = (
            jnp.einsum("kgts,tkgd->skd", prob_low, delta_mixed, preferred_element_type=jnp.float32)
            .reshape(GROUP_SLOTS, kv_cols)
            .astype(jnp.bfloat16)
        )
        row_inner = jnp.sum(prob_exact * delta_prob, axis=-1, keepdims=True)
        delta_raw = (
            jnp.where(allowed[None, None], prob_exact * (delta_prob - row_inner), 0.0)
            * (1.0 - tanh_part * tanh_part)
        ).astype(jnp.bfloat16)
        delta_queries = jnp.einsum(
            "kgts,skd->tkgd", delta_raw, key_vectors, preferred_element_type=jnp.float32
        ).reshape(GROUP_SLOTS, -1, HEAD_SIZE) * HEAD_SIZE ** (-0.5)
        delta_query_proj = (
            apply_rotary(delta_queries, rotary_cosines, -rotary_sines)
            .reshape(GROUP_SLOTS, query_cols)
            .astype(jnp.bfloat16)
        )
        delta_keys = jnp.einsum(
            "kgts,tkgd->skd", delta_raw, query_rows_rotated, preferred_element_type=jnp.float32
        )
        delta_key_proj = (
            apply_rotary(delta_keys, rotary_cosines, -rotary_sines)
            .reshape(GROUP_SLOTS, kv_cols)
            .astype(jnp.bfloat16)
        )
        delta_mixed_proj = jnp.concatenate([delta_query_proj, delta_key_proj, delta_values], axis=1)
        partial_mixed = narrow(contract_first(normed_full, delta_mixed_proj))
        return partial_mixed, contract_last(delta_mixed_proj, mixed_full)

    moments = (
        moment_query,
        moment_key,
        moment_value,
        moment_out,
        moment_gate,
        moment_up,
        moment_down,
    )
    grads, states, updates, delta_normed = ways.close(
        partial_out, attention_backward, (total_down, total_gate, total_up), moments
    )
    in_back, gain_in = norm_backward(inputs, inverse_in, norm_gains[0], delta_normed)
    input_grad = delta_middle + in_back
    gain_grads = ways.finish_gains(jnp.stack([gain_in, gain_attn, gain_mid, gain_feed]))
    return (
        ways.features_out(block_output),
        ways.features_out(input_grad),
        ways.features_out(gain_grads),
        *grads,
        *states,
        *updates,
    )


def solution(mesh):
    sizes = dict(mesh.shape)
    if sizes == {"dp": 8, "tensor": 4}:
        mesh = Mesh(mesh.devices.reshape(4, 2, 2, 2), ("z", "x", "y", "c"))
        ways = Grid(dict(mesh.shape))
    else:
        ways = Plain(sizes)
    token_spec, weight_spec = ways.token_spec, ways.weight_spec
    return jax.shard_map(
        partial(shards, ways),
        mesh=mesh,
        in_specs=(token_spec, token_spec, ways.length_spec, P()) + (weight_spec,) * 14,
        out_specs=(token_spec, token_spec, P()) + (weight_spec,) * 21,
        check_vma=False,
    )
```

```python
from functools import partial

import jax
import jax.numpy as jnp
from jax import lax
from jax.experimental import pallas as pl
from jax.experimental.pallas import tpu as pltpu
from jax.sharding import Mesh
from jax.sharding import PartitionSpec as P

MODEL_WIDTH = 2304
QUERY_HEADS = 8
KEY_VALUE_HEADS = 4
HEAD_SIZE = 256
WINDOW = 4096
BLK = 128
NS_STEPS = 5
GROUP_BLOCKS = 4
GROUP_SLOTS = 512


epsilon = 1e-06
softcap = 50.0
rope_base = 10000.0
coef_first = 3.4445
coef_second = -4.775
coef_third = 2.0315
momentum_decay = 0.95
learn_rate = 0.2
masked_value = -1e30


def slot_layout(lengths):
    blocks = (lengths + BLK - 1) // BLK
    block_ends = jnp.cumsum(blocks, dtype=jnp.int32) * BLK
    slot_index = jnp.arange(GROUP_SLOTS, dtype=jnp.int32)
    passed = slot_index[:, None] >= block_ends[None, :]
    segment = jnp.sum(passed.astype(jnp.int32), axis=1, dtype=jnp.int32)
    before = jnp.sum(jnp.where(passed, blocks[None, :] * BLK, 0), axis=1, dtype=jnp.int32)
    position = slot_index - before
    in_segment = segment[:, None] == jnp.arange(GROUP_BLOCKS, dtype=jnp.int32)[None, :]
    own_length = jnp.sum(jnp.where(in_segment, lengths[None, :], 0), axis=1, dtype=jnp.int32)
    is_alive = position < own_length
    return (segment, position, is_alive)


def allowed_pairs(segment, is_alive):
    slot_index = jnp.arange(GROUP_SLOTS, dtype=jnp.int32)
    distance = slot_index[:, None] - slot_index[None, :]
    same_segment = segment[:, None] == segment[None, :]
    inside = (
        is_alive[:, None] & is_alive[None, :] & same_segment & (distance >= 0) & (distance < WINDOW)
    )
    return (distance == 0) | inside


def rope_tables(position):
    half_width = HEAD_SIZE // 2
    frequency = rope_base ** (-2.0 * jnp.arange(half_width, dtype=jnp.float32) / HEAD_SIZE)
    angles = position.astype(jnp.float32)[:, None] * frequency[None, :]
    return (jnp.cos(angles), jnp.sin(angles))


def apply_rotary(values, rotary_cosines, rotary_sines):
    half_width = HEAD_SIZE // 2
    first_half = values[..., :half_width]
    second_half = values[..., half_width:]
    rotary_cosines = rotary_cosines[:, None, :]
    rotary_sines = rotary_sines[:, None, :]
    return jnp.concatenate(
        [
            first_half * rotary_cosines - second_half * rotary_sines,
            second_half * rotary_cosines + first_half * rotary_sines,
        ],
        axis=-1,
    )


def norm_forward(values, gain):
    inverse = lax.rsqrt(jnp.mean(values * values, axis=-1, keepdims=True) + epsilon)
    return (values * inverse * gain, inverse)


def norm_backward(values, inverse, gain, upstream):
    scaled = upstream * gain
    row_inner = jnp.mean(scaled * values, axis=-1, keepdims=True)
    return (
        inverse * scaled - values * inverse**3 * row_inner,
        jnp.sum(upstream * values * inverse, axis=0),
    )


def contract_last(left_side, right_side):
    return lax.dot_general(
        left_side, right_side, (((1,), (1,)), ((), ())), preferred_element_type=jnp.float32
    )


def contract_first(left_side, right_side):
    return lax.dot_general(
        left_side, right_side, (((0,), (0,)), ((), ())), preferred_element_type=jnp.float32
    )


HALF = HEAD_SIZE // 2

BRIEF = pl.CostEstimate(flops=1024, bytes_accessed=1024, transcendentals=0)


def two_terms(values):
    high = values.astype(jnp.bfloat16)
    low = (values - high.astype(jnp.float32)).astype(jnp.bfloat16)
    return high, low


def product(left_side, right_side):
    return jnp.dot(left_side, right_side, preferred_element_type=jnp.float32)


def product_f32(left_terms, right_terms):
    left_high, left_low = left_terms
    right_high, right_low = right_terms
    return product(left_high, right_high) + (
        product(left_high, right_low) + product(left_low, right_high)
    )


def gram_body(counts, *refs):
    out_ref = refs[-1]
    step = pl.program_id(0)
    start = 0
    for ref, count in zip(refs[:-1], counts):

        @pl.when((step >= start) & (step < start + count))
        def _(ref=ref):
            high, low = two_terms(ref[...])
            mixed = contract_first(high, low)
            gram = contract_first(high, high) + (mixed + mixed.T)
            out_ref[0, 0] = gram[:HALF, :HALF]
            out_ref[0, 1] = gram[:HALF, HALF:]
            out_ref[0, 2] = gram[HALF:, HALF:]

        start += count

    @pl.when(step >= start)
    def _():
        out_ref[...] = jnp.zeros(out_ref.shape, out_ref.dtype)


def clamped(start, count):
    return lambda step: (0, jnp.clip(step - start, 0, count - 1))


def spans(states):
    counts = [state.shape[1] // HEAD_SIZE for state in states]
    starts = [sum(counts[:i]) for i in range(len(counts))]
    return counts, starts


def grams(states, slots):
    counts, starts = spans(states)
    rows = states[0].shape[0]
    return pl.pallas_call(
        partial(gram_body, counts),
        grid=(slots,),
        in_specs=[
            pl.BlockSpec((rows, HEAD_SIZE), clamped(s, c)) for s, c in zip(starts, counts)
        ],
        out_specs=pl.BlockSpec((1, 3, HALF, HALF), lambda step: (step, 0, 0, 0)),
        out_shape=jax.ShapeDtypeStruct((slots, 3, HALF, HALF), jnp.float32),
        cost_estimate=BRIEF,
        compiler_params=pltpu.CompilerParams(vmem_limit_bytes=40 * 1024 * 1024),
    )(*states)


def add_gram(out_ref, index, values):
    high, low = two_terms(values)
    mixed = contract_first(high, low)
    gram = contract_first(high, high) + (mixed + mixed.T)
    out_ref[index, 0] += gram[:HALF, :HALF]
    out_ref[index, 1] += gram[:HALF, HALF:]
    out_ref[index, 2] += gram[HALF:, HALF:]


def inner_body(total_ref, moment_ref, out_ref):
    out_ref[...] = jnp.zeros(out_ref.shape, out_ref.dtype)
    gradient = total_ref[...].astype(jnp.float32)
    add_gram(out_ref, 0, momentum_decay * moment_ref[...].astype(jnp.float32) + gradient)


def inner_grams(total, moment, blocks, first):
    rows = total.shape[0]
    return pl.pallas_call(
        inner_body,
        grid=(blocks,),
        in_specs=[
            pl.BlockSpec((rows, HEAD_SIZE), lambda step: (0, step)),
            pl.BlockSpec((rows, HEAD_SIZE), lambda step: (0, step + first)),
        ],
        out_specs=pl.BlockSpec((1, 3, HALF, HALF), lambda step: (step, 0, 0, 0)),
        out_shape=jax.ShapeDtypeStruct((blocks, 3, HALF, HALF), jnp.float32),
        cost_estimate=BRIEF,
        compiler_params=pltpu.CompilerParams(vmem_limit_bytes=40 * 1024 * 1024),
    )(total, moment)


ROW_TILE = 96


def finish_body(main, place_ref, *refs):
    depth = len(refs) - 4
    moment_ref, grad_ref, state_ref, gram_ref = refs[depth:]
    rest = refs[0].shape[1] - main
    for j in range(depth):
        turn = lax.rem(place_ref[0] + depth - j, depth)
        for k in range(depth):

            @pl.when(turn == k)
            def _(piece=refs[k], j=j):
                grad_ref[:, main * j : main * (j + 1)] = piece[:, :main].astype(jnp.float32)
                start = main * depth + rest * j
                grad_ref[:, start : start + rest] = piece[:, main:].astype(jnp.float32)

    state_ref[...] = momentum_decay * moment_ref[...] + grad_ref[...]

    @pl.when(pl.program_id(0) == 0)
    def _():
        gram_ref[...] = jnp.zeros(gram_ref.shape, gram_ref.dtype)

    add_gram(gram_ref, 0, state_ref[:, main * depth :])


def finish(pieces, position, moment, main):
    rows, cols = moment.shape
    wide_spec = pl.BlockSpec((ROW_TILE, cols), lambda step, place: (step, 0))
    piece_spec = pl.BlockSpec((ROW_TILE, pieces[0].shape[1]), lambda step, place: (step, 0))
    return pl.pallas_call(
        partial(finish_body, main),
        grid_spec=pltpu.PrefetchScalarGridSpec(
            num_scalar_prefetch=1,
            grid=(rows // ROW_TILE,),
            in_specs=[piece_spec] * len(pieces) + [wide_spec],
            out_specs=[
                wide_spec,
                wide_spec,
                pl.BlockSpec((1, 3, HALF, HALF), lambda step, place: (0, 0, 0, 0)),
            ],
        ),
        out_shape=[
            jax.ShapeDtypeStruct((rows, cols), jnp.float32),
            jax.ShapeDtypeStruct((rows, cols), jnp.float32),
            jax.ShapeDtypeStruct((1, 3, HALF, HALF), jnp.float32),
        ],
        cost_estimate=BRIEF,
        compiler_params=pltpu.CompilerParams(vmem_limit_bytes=40 * 1024 * 1024),
    )(position.reshape(1), *pieces, moment)


def attn_finish_body(depth, *refs):
    sums = refs[: 2 * depth]
    moments, grads, states = (refs[2 * depth + 4 * i : 2 * depth + 4 * i + 4] for i in range(3))
    gram_ref = refs[-1]

    @pl.when(pl.program_id(0) == 0)
    def _():
        gram_ref[...] = jnp.zeros(gram_ref.shape, gram_ref.dtype)

    mixed = sum(ref[...].astype(jnp.float32) for ref in sums[:depth])
    out = sum(ref[...].astype(jnp.float32) for ref in sums[depth:])
    slot = 0
    start = 0
    for moment_ref, grad_ref, state_ref in zip(moments, grads, states):
        cols = moment_ref.shape[1]
        if grad_ref is grads[-1]:
            gradient = out
        else:
            gradient = mixed[:, start : start + cols]
        start += cols
        grad_ref[...] = gradient
        state = momentum_decay * moment_ref[...] + gradient
        state_ref[...] = state
        for block in range(cols // HEAD_SIZE):
            add_gram(gram_ref, slot, state[:, block * HEAD_SIZE : (block + 1) * HEAD_SIZE])
            slot += 1


def attn_finish(mixed, out, moments, slots):
    rows = moments[0].shape[0]

    def spec(v):
        return pl.BlockSpec((ROW_TILE, v.shape[1]), lambda step: (step, 0))

    outs = [jax.ShapeDtypeStruct(m.shape, jnp.float32) for m in moments]
    results = pl.pallas_call(
        partial(attn_finish_body, len(mixed)),
        grid=(rows // ROW_TILE,),
        in_specs=[spec(v) for v in (*mixed, *out, *moments)],
        out_specs=[spec(v) for v in outs + outs]
        + [pl.BlockSpec((slots, 3, HALF, HALF), lambda step: (0, 0, 0, 0))],
        out_shape=outs + outs + [jax.ShapeDtypeStruct((slots, 3, HALF, HALF), jnp.float32)],
        cost_estimate=BRIEF,
        compiler_params=pltpu.CompilerParams(vmem_limit_bytes=40 * 1024 * 1024),
    )(*mixed, *out, *moments)
    return list(results[:4]), list(results[4:8]), results[8]


def newton_body(count, *refs):
    out_ref = refs[-1]
    row = lax.broadcasted_iota(jnp.int32, (HEAD_SIZE, HEAD_SIZE), 0)
    col = lax.broadcasted_iota(jnp.int32, (HEAD_SIZE, HEAD_SIZE), 1)
    unit = (row == col).astype(jnp.float32)
    squares = []
    scales = []
    for i in range(count):
        parts = [sum(ref[i, j].astype(jnp.float32) for ref in refs[:-1]) for j in range(3)]
        gram = jnp.concatenate(
            [
                jnp.concatenate([parts[0], parts[1]], axis=1),
                jnp.concatenate([parts[1].T, parts[2]], axis=1),
            ],
            axis=0,
        )
        total = jnp.sum(jnp.sum(gram * unit, axis=1, keepdims=True), axis=0, keepdims=True)
        inverse = 1.0 / (jnp.sqrt(total) + 1e-07)
        squares.append(gram * inverse * inverse)
        scales.append(-learn_rate * (MODEL_WIDTH / HEAD_SIZE) ** 0.5 * inverse)
    totals = [None] * count
    for repeat in range(NS_STEPS):
        terms = [two_terms(square) for square in squares]
        seconds = [product_f32(t, t) for t in terms]
        steps = [
            coef_first * unit + (coef_second * square + coef_third * second)
            for square, second in zip(squares, seconds)
        ]
        step_terms = [two_terms(step) for step in steps]
        if repeat == 0:
            totals = steps
        else:
            totals = [
                product_f32(two_terms(total), s) for total, s in zip(totals, step_terms)
            ]
        if repeat < NS_STEPS - 1:
            inner = [product_f32(s, t) for s, t in zip(step_terms, terms)]
            squares = [product_f32(two_terms(v), s) for v, s in zip(inner, step_terms)]
    for i in range(count):
        result = (totals[i] * scales[i]).astype(out_ref.dtype)
        out_ref[i, 0] = result[:HALF, :HALF]
        out_ref[i, 1] = result[:HALF, HALF:]
        out_ref[i, 2] = result[HALF:, HALF:]


def newton(pieces):
    count = pieces[0].shape[0]
    return pl.pallas_call(
        partial(newton_body, count),
        out_shape=jax.ShapeDtypeStruct((count, 3, HALF, HALF), jnp.bfloat16),
        cost_estimate=BRIEF,
        compiler_params=pltpu.CompilerParams(vmem_limit_bytes=40 * 1024 * 1024),
    )(*pieces)


def apply_body(state_ref, factor_ref, *refs):
    out_ref = refs[-1]
    upper = factor_ref[0, 1].astype(jnp.float32)
    factor = jnp.concatenate(
        [
            jnp.concatenate([factor_ref[0, 0], factor_ref[0, 1]], axis=1),
            jnp.concatenate([upper.T.astype(jnp.bfloat16), factor_ref[0, 2]], axis=1),
        ],
        axis=0,
    )
    high, low = two_terms(state_ref[...])
    out_ref[...] = product(high, factor) + product(low, factor)


def apply_factor(state, factors, start, low=0, high=None, into=None):
    rows, cols = state.shape
    high = cols // HEAD_SIZE if high is None else high
    block = pl.BlockSpec((rows, HEAD_SIZE), lambda step: (0, step + low))
    return pl.pallas_call(
        apply_body,
        grid=(high - low,),
        in_specs=[block, pl.BlockSpec((1, 3, HALF, HALF), lambda step: (step + start, 0, 0, 0))]
        + ([] if into is None else [pl.BlockSpec(memory_space=pl.ANY)]),
        out_specs=block,
        out_shape=jax.ShapeDtypeStruct((rows, cols), jnp.float32),
        input_output_aliases={} if into is None else {2: 0},
        cost_estimate=BRIEF,
        compiler_params=pltpu.CompilerParams(vmem_limit_bytes=40 * 1024 * 1024),
    )(state, factors, *([] if into is None else [into]))


VMEM_BYTES = 50 * 1024 * 1024


def dense_call(body, grid, in_specs, out_specs, out_shape, *operands):
    return pl.pallas_call(
        body,
        grid=grid,
        in_specs=in_specs,
        out_specs=out_specs,
        out_shape=out_shape,
        cost_estimate=BRIEF,
        compiler_params=pltpu.CompilerParams(vmem_limit_bytes=VMEM_BYTES),
    )(*operands)


def column_tile(width):
    return width if width % 768 else 768


def enter_body(rows_ref, gate_ref, up_ref, hidden_ref, gelu_ref, pull_ref):
    rows = rows_ref[...]
    factor = (2.0 / jnp.pi) ** 0.5
    for p in range(gate_ref.shape[0]):
        gate = product(rows, gate_ref[p])
        up = product(rows, up_ref[p])
        squared = gate * gate
        bend = jnp.tanh(factor * (gate + 0.044715 * gate * squared))
        upper = 0.5 * (1.0 + bend)
        gelu = gate * upper
        slope = upper + 0.5 * gate * (1.0 - bend * bend) * (factor * (1.0 + 0.134145 * squared))
        hidden_ref[p] = (gelu * up).astype(jnp.bfloat16)
        gelu_ref[p] = gelu.astype(jnp.bfloat16)
        pull_ref[p] = (up * slope).astype(jnp.bfloat16)


def enter(rows, gate, up):
    count, width = rows.shape
    pieces, _, cols = gate.shape
    tile = column_tile(cols)
    weight = pl.BlockSpec((pieces, width, tile), lambda j, i: (0, 0, j))
    out = pl.BlockSpec((pieces, 256, tile), lambda j, i: (0, i, j))
    return dense_call(
        enter_body,
        (cols // tile, count // 256),
        [pl.BlockSpec((256, width), lambda j, i: (i, 0)), weight, weight],
        [out] * 3,
        [jax.ShapeDtypeStruct((pieces, count, cols), jnp.bfloat16)] * 3,
        rows,
        gate,
        up,
    )


def leave_body(rows_ref, down_ref, gelu_ref, pull_ref, gate_ref, up_ref):
    rows = rows_ref[...]
    for p in range(down_ref.shape[0]):
        delta = product(rows, down_ref[p])
        gate_ref[p] = (delta * pull_ref[p].astype(jnp.float32)).astype(jnp.bfloat16)
        up_ref[p] = (delta * gelu_ref[p].astype(jnp.float32)).astype(jnp.bfloat16)


def leave(rows, down, gelu, pull):
    count, width = rows.shape
    pieces, _, cols = down.shape
    tile = column_tile(cols)
    out = pl.BlockSpec((pieces, 256, tile), lambda j, i: (0, i, j))
    return dense_call(
        leave_body,
        (cols // tile, count // 256),
        [
            pl.BlockSpec((256, width), lambda j, i: (i, 0)),
            pl.BlockSpec((pieces, width, tile), lambda j, i: (0, 0, j)),
            out,
            out,
        ],
        [out] * 2,
        [jax.ShapeDtypeStruct((pieces, count, cols), jnp.bfloat16)] * 2,
        rows,
        down,
        gelu,
        pull,
    )


def shrink_body(count, *refs):
    pieces = refs[0].shape[0]
    total = None
    for i in range(count):
        for p in range(pieces):
            term = contract_last(refs[i][p], refs[count + i][p])
            total = term if total is None else total + term
    refs[-1][...] = total.astype(refs[-1].dtype)


def shrink(lefts, rights, rows, part, dtype):
    pieces, width, cols = rights[0].shape
    count = len(lefts)
    tile = 768 if cols < 768 else 256
    return dense_call(
        partial(shrink_body, count),
        (width // tile,),
        [pl.BlockSpec((pieces, rows, cols), lambda j: (0, part, 0))] * count
        + [pl.BlockSpec((pieces, tile, cols), lambda j: (0, j, 0))] * count,
        pl.BlockSpec((rows, tile), lambda j: (0, j)),
        jax.ShapeDtypeStruct((rows, width), dtype),
        *lefts,
        *rights,
    )


def outer_body(left_ref, right_ref, out_ref):
    left = left_ref[...]
    for p in range(out_ref.shape[0]):
        out_ref[p] = contract_first(left, right_ref[p]).astype(jnp.bfloat16)


def outer(left, right):
    rows, width = left.shape
    pieces, _, cols = right.shape
    tile = 384 if cols < 768 else 256
    return dense_call(
        outer_body,
        (width // tile,),
        [
            pl.BlockSpec((rows, tile), lambda j: (0, j)),
            pl.BlockSpec((pieces, rows, cols), lambda j: (0, 0, 0)),
        ],
        pl.BlockSpec((pieces, tile, cols), lambda j: (0, j, 0)),
        jax.ShapeDtypeStruct((pieces, width, cols), jnp.bfloat16),
        left,
        right,
    )


def rotated(values, cosines, sines):
    first, second = values[:, :HALF], values[:, HALF:]
    return jnp.concatenate(
        [first * cosines - second * sines, second * cosines + first * sines], axis=1
    )


def head(index):
    return slice(index * HEAD_SIZE, (index + 1) * HEAD_SIZE)


def pair_mask(segment_rows, segment_cols, alive_rows, alive_cols):
    shape = (segment_rows.shape[0], segment_cols.shape[1])
    distance = lax.broadcasted_iota(jnp.int32, shape, 0) - lax.broadcasted_iota(
        jnp.int32, shape, 1
    )
    inside = (
        (alive_rows * alive_cols > 0)
        & (segment_rows == segment_cols)
        & (distance >= 0)
        & (distance < WINDOW)
    )
    return (distance == 0) | inside


def attend_body(kv_heads, width, *refs):
    projected, cosines, sines = (ref[...] for ref in refs[:3])
    query_ref, key_ref, value_ref, prob_ref, tanh_ref, mixed_ref = refs[7:]
    allowed = pair_mask(*(ref[...] for ref in refs[3:7]))
    query_heads = kv_heads * width
    for j in range(kv_heads):
        key = rotated(projected[:, head(query_heads + j)], cosines, sines).astype(jnp.bfloat16)
        value = projected[:, head(query_heads + kv_heads + j)].astype(jnp.bfloat16)
        key_ref[:, head(j)] = key
        value_ref[:, head(j)] = value
        for i in range(j * width, (j + 1) * width):
            query = rotated(projected[:, head(i)], cosines, sines) * HEAD_SIZE ** (-0.5)
            query = query.astype(jnp.bfloat16)
            query_ref[:, head(i)] = query
            tanh_part = jnp.tanh(contract_last(query, key) / softcap)
            masked = jnp.where(allowed, softcap * tanh_part, masked_value)
            exponent = jnp.exp(masked - jnp.max(masked, axis=-1, keepdims=True))
            prob = exponent / jnp.sum(exponent, axis=-1, keepdims=True)
            prob_ref[i] = prob
            tanh_ref[i] = tanh_part
            mixed_ref[:, head(i)] = product(prob.astype(jnp.bfloat16), value).astype(jnp.bfloat16)


def attend_back_body(kv_heads, width, *refs):
    delta_mixed, cosines, sines = (ref[...] for ref in refs[:3])
    query_ref, key_ref, value_ref, prob_ref, tanh_ref, out_ref = refs[7:]
    allowed = pair_mask(*(ref[...] for ref in refs[3:7]))
    query_heads = kv_heads * width
    for j in range(kv_heads):
        key, value = key_ref[:, head(j)], value_ref[:, head(j)]
        delta_key = delta_value = None
        for i in range(j * width, (j + 1) * width):
            delta = delta_mixed[:, head(i)]
            prob, tanh_part = prob_ref[i], tanh_ref[i]
            delta_prob = contract_last(delta, value)
            inner = jnp.sum(prob * delta_prob, axis=-1, keepdims=True)
            raw = jnp.where(allowed, prob * (delta_prob - inner), 0.0)
            raw = (raw * (1.0 - tanh_part * tanh_part)).astype(jnp.bfloat16)
            delta_query = product(raw, key) * HEAD_SIZE ** (-0.5)
            out_ref[:, head(i)] = rotated(delta_query, cosines, -sines).astype(jnp.bfloat16)
            key_term = contract_first(raw, query_ref[:, head(i)])
            value_term = contract_first(prob.astype(jnp.bfloat16), delta)
            delta_key = key_term if delta_key is None else delta_key + key_term
            delta_value = value_term if delta_value is None else delta_value + value_term
        out_ref[:, head(query_heads + j)] = rotated(delta_key, cosines, -sines).astype(
            jnp.bfloat16
        )
        out_ref[:, head(query_heads + kv_heads + j)] = delta_value.astype(jnp.bfloat16)


def whole_call(body, out_shape, *operands):
    return pl.pallas_call(
        body,
        out_shape=out_shape,
        cost_estimate=BRIEF,
        compiler_params=pltpu.CompilerParams(vmem_limit_bytes=VMEM_BYTES),
    )(*operands)


def fence(*values):
    return lax.optimization_barrier(values)


def after(value, *others):
    return lax.optimization_barrier((value,) + others)[0]


class Plain:
    def __init__(self, sizes):
        self.owners = sizes["dp"]
        self.token_spec = P(("dp", "tensor"), None)
        self.length_spec = P("dp", None)
        self.weight_spec = P("dp", "tensor")
        self.every = ("dp", "tensor")

    def setup(self):
        self.part = lax.axis_index("tensor")

    def gather_dp(self, shard):
        return lax.all_gather(shard, "dp", axis=0, tiled=True)

    def scatter_dp(self, partial_sum):
        return wide(lax.psum_scatter(partial_sum, "dp", scatter_dimension=0, tiled=True))

    def open(self, normed, mixed, out, gate, up, down, moments):
        self.later = {"up": up, "down": down}
        return (
            self.attn_rows(normed),
            self.gather_dp(mixed),
            self.gather_dp(out),
            self.gather_dp(gate)[None],
        )

    def beside_attention(self, values):
        return values, self.gather_dp(self.later["up"])[None]

    def beside_sum(self, values):
        return self.attn_sum(values)

    def beside_rows(self, values):
        return self.attn_rows(values)

    def beside_hidden(self, values):
        return values, self.gather_dp(self.later["down"])[None]

    def attn_rows(self, values):
        return lax.all_gather(values, "tensor", axis=0, tiled=True)

    def attn_sum(self, values):
        return lax.psum_scatter(values, "tensor", scatter_dimension=0, tiled=True)

    def features_in(self, values):
        return values

    def features_out(self, values):
        return values

    def mlp_sum_rows(self, partial_sums):
        return self.scatter_dp(partial_sums[0])

    def close(self, partial_out, attention_backward, totals, moments, end_norm):
        partial_mixed, partial_normed = attention_backward(partial_out)
        cuts = (moments[0].shape[1], moments[0].shape[1] + moments[1].shape[1])
        grads = jnp.split(self.scatter_dp(partial_mixed), cuts, axis=1)
        grads = (*grads, self.scatter_dp(partial_out), totals[1], totals[2], totals[0])
        states = [momentum_decay * m + g for m, g in zip(moments, grads)]
        first = muon(self, states[6:] + states[4:5])
        last = muon(self, states[5:6] + states[:4])
        updates = (*last[1:], first[1], last[0], first[0])
        input_grad, gains = end_norm(self.attn_sum(partial_normed))
        return grads, states, updates, input_grad, self.sum_every(gains)

    def sum_every(self, values):
        return lax.psum(values, self.every)

    def mlp_rows(self, values):
        return self.attn_rows(values)

    def mlp_sum(self, lefts, rights):
        values = shrink(lefts, rights, lefts[0].shape[1], 0, jnp.float32)
        return self.attn_sum(values), values

    def attn_rows_beside(self, values):
        return self.attn_rows(values)

    def gram_sum(self, values):
        return [lax.psum_scatter(values, "dp", scatter_dimension=0, tiled=True)]

    def factor_gather(self, values):
        return lax.all_gather(values, "dp", axis=0, tiled=True)


def shift(values, axis, distance):
    size = lax.axis_size(axis)
    return lax.ppermute(values, axis, [(i, (i + distance) % size) for i in range(size)])


def pick(stacked, index):
    return lax.dynamic_index_in_dim(stacked, index, 0, keepdims=False)


def wide(values):
    return values.astype(jnp.float32)


def narrow(values):
    return values.astype(jnp.bfloat16)


def place(buffer, values, *index):
    fresh = values.reshape((1,) * len(index) + values.shape)
    zero = jnp.zeros((), jnp.int32)
    return lax.dynamic_update_slice(buffer, fresh, tuple(index) + (zero,) * values.ndim)


class Grid:
    def __init__(self, sizes):
        self.depth = sizes["z"]
        self.owners = sizes["z"] * sizes["x"]
        self.token_spec = P(("z", "x", "y", "c"), None)
        self.length_spec = P(("z", "x"), None)
        self.weight_spec = P(("z", "x"), ("y", "c"))
        self.every = ("z", "x", "y", "c")

    def setup(self):
        self.z, self.x, self.y, self.c = (lax.axis_index(a) for a in self.every)
        self.part = self.y * 2 + self.c


    def features_in(self, values):
        split = values.reshape(values.shape[:-1] + (self.depth, 2, -1))
        return jnp.swapaxes(split, -3, -2).reshape(values.shape)

    def features_out(self, values):
        split = values.reshape(values.shape[:-1] + (2, self.depth, -1))
        return jnp.swapaxes(split, -3, -2).reshape(values.shape)

    def back(self, distance):
        return lax.rem(self.z + self.depth - distance, self.depth)

    def ahead(self, distance):
        return lax.rem(self.z + distance, self.depth)

    def open(self, normed, mixed, out, gate, up, down, moments):
        attn = jnp.concatenate([mixed, out], axis=1)
        line = [attn, shift(attn, "z", 1)]
        across = [shift(attn, "x", 1)]
        over = shift(normed, "y", 1)
        across[0], line[1], over, gate, up = fence(across[0], line[1], over, gate, up)

        across.append(shift(line[1], "x", 1))
        line.append(shift(line[1], "z", 1))
        pair = shift(jnp.concatenate([normed, over], axis=0), "c", 1)
        gate_sent = self.send(self.quarters(gate))
        across[1], line[2], pair, up, down, *gate_sent = fence(
            across[1], line[2], pair, up, down, *gate_sent
        )

        across.append(shift(line[2], "x", 1))
        line.append(shift(line[2], "z", 1))
        up_sent = self.send(self.quarters(up))
        across[2], line[3], down, gate_sent, up_sent, moments = lax.optimization_barrier(
            (across[2], line[3], down, gate_sent, up_sent, moments)
        )

        across.append(shift(line[3], "x", 1))
        gate_arrived = self.arrive(gate_sent)
        down_sent = self.send(self.quarters(down))
        across[3], gate_arrived, up_sent, down_sent, moments = lax.optimization_barrier(
            (across[3], gate_arrived, up_sent, down_sent, moments)
        )
        self.up_sent, self.down_sent, self.moments = up_sent, down_sent, moments

        mixed_cols = mixed.shape[1]
        full = jnp.zeros((2, self.depth) + attn.shape, attn.dtype)
        for k in range(self.depth):
            full = place(full, line[k], self.x, self.back(k))
            full = place(full, across[k], 1 - self.x, self.back(k))
        full, gate_column = fence(full.reshape((-1,) + attn.shape[1:]), self.column(gate_arrived))
        return (
            self.order_rows(normed, over, pair),
            full[:, :mixed_cols],
            full[:, mixed_cols:],
            self.gather_plane(gate_column),
        )

    def beside_attention(self, values):
        arrived = self.arrive(self.up_sent)
        values, arrived, down_sent = lax.optimization_barrier((values, arrived, self.down_sent))
        values, column, moments, down_sent = lax.optimization_barrier(
            (values, self.column(arrived), self.moments, down_sent)
        )
        self.down_sent, self.moments = down_sent, moments
        return values, self.gather_plane(column)

    def beside_sum(self, values):
        kept, sent = self.core_half(values)
        received = shift(sent, "c", 1)
        arrived = self.arrive(self.down_sent)
        mine = kept + wide(received)
        total = pick(mine, self.y) + wide(shift(narrow(pick(mine, 1 - self.y)), "y", 1))
        total, arrived = lax.optimization_barrier((total, arrived))
        total, column, moments = lax.optimization_barrier(
            (total, self.column(arrived), self.moments)
        )
        self.down_full = self.gather_plane(column)
        self.moments = moments
        return total

    def beside_rows(self, values):
        values, moments = lax.optimization_barrier((values, self.moments))
        line = [shift(values, "z", k) for k in range(1, self.depth)]
        inner = [self.main_quarters(narrow(m)) for m in moments]
        inner_sent = [
            self.send(jnp.concatenate([inner[0], inner[1]], axis=2)),
            self.send(inner[2]),
        ]
        line, inner_sent = lax.optimization_barrier((line, inner_sent))
        line = jnp.concatenate(line, axis=0)
        pair = shift(values, "c", 1), shift(line, "c", 1)
        values, line, pair, inner_sent = lax.optimization_barrier((values, line, pair, inner_sent))
        self.inner_sent = inner_sent
        return jnp.concatenate([values, line, *pair], axis=0)

    def beside_hidden(self, values):
        arrived = self.arrive(self.inner_sent[0])
        values, arrived = lax.optimization_barrier((values, arrived))
        self.inner = self.column(arrived).reshape(-1, 2 * self.main)
        return values, self.down_full


    def main_quarters(self, shard):
        rows, cols = shard.shape
        self.main = cols // (self.depth * HEAD_SIZE) * HEAD_SIZE
        main = shard[:, : self.depth * self.main]
        return main.reshape(rows, self.depth, self.main).transpose(1, 0, 2)

    def quarters(self, shard):
        main = self.main_quarters(shard)
        rest = shard[:, self.depth * self.main :]
        rest = rest.reshape(shard.shape[0], self.depth, -1).transpose(1, 0, 2)
        return jnp.concatenate([main, rest], axis=2)

    def send(self, chunks):
        return [pick(chunks, self.ahead(k)) for k in range(self.depth)]

    def arrive(self, sent):
        return [sent[0]] + [shift(sent[k], "z", k) for k in range(1, self.depth)]

    def column(self, arrived):
        column = jnp.zeros((self.depth,) + arrived[0].shape, arrived[0].dtype)
        for k, values in enumerate(arrived):
            column = place(column, values, self.back(k))
        return column

    def gather_plane(self, column):
        full = lax.all_gather(column, ("y", "x"), axis=0, tiled=True)
        return full.reshape(2, 2 * self.depth * column.shape[1], -1)

    def order_rows(self, own, over, pair):
        rows = own.shape[0]
        near, far = pair[:rows], pair[rows:]
        first = self.y == 0
        low_own, high_own = jnp.where(first, own, over), jnp.where(first, over, own)
        low_near, high_near = jnp.where(first, near, far), jnp.where(first, far, near)
        core = self.c == 0
        return jnp.concatenate(
            [
                jnp.where(core, low_own, low_near),
                jnp.where(core, low_near, low_own),
                jnp.where(core, high_own, high_near),
                jnp.where(core, high_near, high_own),
            ],
            axis=0,
        )

    def attn_rows(self, values):
        over = shift(values, "y", 1)
        pair = shift(jnp.concatenate([values, over], axis=0), "c", 1)
        return self.order_rows(values, over, pair)

    def core_half(self, values):
        stacked = values.reshape(2, 2, -1, values.shape[1]).transpose(1, 0, 2, 3)
        return pick(stacked, self.c), narrow(pick(stacked, 1 - self.c))

    def attn_sum(self, values):
        kept, sent = self.core_half(values)
        mine = kept + wide(shift(sent, "c", 1))
        return pick(mine, self.y) + wide(shift(narrow(pick(mine, 1 - self.y)), "y", 1))

    def mlp_sum_rows(self, partial_sums):
        stacked = partial_sums.reshape(4 * self.depth, -1, partial_sums.shape[-1])
        return lax.psum_scatter(stacked, ("y", "x"), scatter_dimension=0, tiled=True)

    def mlp_rows(self, values):
        line = jnp.concatenate([shift(values, "z", k) for k in range(1, self.depth)], axis=0)
        return jnp.concatenate([values, line, shift(values, "c", 1), shift(line, "c", 1)], axis=0)

    def mlp_sum(self, lefts, rights):
        rows = lefts[0].shape[1] // 2
        away = shrink(lefts, rights, rows, 1, jnp.bfloat16)
        received = shift(away, "c", 1)
        kept = shrink([after(v, away) for v in lefts], rights, rows, 0, jnp.bfloat16)
        mine = (wide(kept) + wide(received)).reshape(self.depth, -1, kept.shape[1])
        sent = [narrow(mine[k]) for k in range(1, self.depth)]
        own, *sent = fence(mine[0], *sent)
        arrived = [shift(v, "z", self.depth - k) for k, v in enumerate(sent, 1)]
        return own + sum(wide(v) for v in arrived), own

    def attn_rows_beside(self, values):
        values, sent = lax.optimization_barrier((values, self.inner_sent[1]))
        arrived = self.arrive(sent)
        over = shift(values, "y", 1)
        values, over, arrived = lax.optimization_barrier((values, over, arrived))
        self.inner_last = arrived
        pair = shift(jnp.concatenate([values, over], axis=0), "c", 1)
        return self.order_rows(values, over, pair)

    def halves(self, values):
        stacked = values.reshape((2, -1) + values.shape[1:])
        return pick(stacked, self.x), pick(stacked, 1 - self.x)

    def main_grams(self, total, inner, first):
        blocks = self.main // HEAD_SIZE
        rows = total.reshape(-1, total.shape[-1])
        return self.halves(inner_grams(rows, inner, blocks, first * blocks))

    def close(self, partial_out, attention_backward, totals, moments, end_norm):
        total_down, total_gate, total_up = totals

        stacked = partial_out.reshape(2, -1, partial_out.shape[1])
        kept_out, sent_out = pick(stacked, self.x), pick(stacked, 1 - self.x)
        partial_out, sent_out, down_sent = lax.optimization_barrier(
            (partial_out, sent_out, self.send(total_down))
        )
        received = shift(sent_out, "x", 1)
        turned_down = self.arrive(down_sent)
        partial_mixed, partial_normed = attention_backward(partial_out)
        partial_mixed, partial_normed, received, turned_down, total_gate = (
            lax.optimization_barrier(
                (partial_mixed, partial_normed, received, turned_down, total_gate)
            )
        )
        out_rows = (wide(kept_out) + wide(received)).reshape(self.depth, -1, kept_out.shape[1])
        out_sent = self.send(narrow(out_rows))
        gate_sent = self.send(total_gate)
        stacked = partial_mixed.reshape(2, -1, partial_mixed.shape[1])
        kept_mixed, sent_mixed = pick(stacked, self.x), pick(stacked, 1 - self.x)
        kept_normed, sent_normed = self.core_half(partial_normed)
        out_sent, gate_sent, sent_mixed, sent_normed = lax.optimization_barrier(
            (out_sent, gate_sent, sent_mixed, sent_normed)
        )

        received = shift(sent_mixed, "x", 1)
        out_arrived = self.arrive(out_sent)
        turned_gate = self.arrive(gate_sent)
        normed_received = shift(sent_normed, "c", 1)
        kept_down, sent_down = self.main_grams(total_down, self.inner, 0)
        kept_gate, sent_gate = self.main_grams(total_gate, self.inner, 1)
        sent_grams = jnp.concatenate([sent_down, sent_gate])
        received, out_arrived, turned_gate, normed_received, sent_grams, turned_down = (
            lax.optimization_barrier(
                (
                    received,
                    out_arrived,
                    turned_gate,
                    normed_received,
                    sent_grams,
                    turned_down,
                )
            )
        )

        mixed_rows = (wide(kept_mixed) + wide(received)).reshape(
            self.depth, -1, kept_mixed.shape[1]
        )
        mixed_arrived = self.arrive(self.send(narrow(mixed_rows)))
        received_grams = shift(sent_grams, "x", 1)
        mine = kept_normed + wide(normed_received)
        normed_received = shift(narrow(pick(mine, 1 - self.y)), "y", 1)
        finished_down = finish(turned_down, self.z, moments[6], self.main)
        finished_gate = finish(turned_gate, self.z, moments[4], self.main)
        inner_last = self.column(self.inner_last).reshape(-1, self.main)
        mixed_arrived, received_grams, normed_received, inner_last, total_up = (
            lax.optimization_barrier(
                (mixed_arrived, received_grams, normed_received, inner_last, total_up)
            )
        )
        input_grad, gains = end_norm(pick(mine, self.y) + wide(normed_received))

        turned_up = self.arrive(self.send(total_up))
        kept_last, sent_last = self.main_grams(total_up, inner_last, 0)
        received_last = shift(sent_last, "x", 1)
        grads, states, attn_grams = attn_finish(
            mixed_arrived, out_arrived, moments[:4], self.owners
        )
        kept_attn, sent_attn = self.halves(attn_grams)
        received_attn = shift(sent_attn, "x", 1)
        main_factors = newton([jnp.concatenate([kept_down, kept_gate]), received_grams])
        turned_up, received_attn, received_last, main_factors, gains = lax.optimization_barrier(
            (turned_up, received_attn, received_last, main_factors, gains)
        )

        attn_arrived = self.arrive(self.send((kept_attn + received_attn)[:, None]))
        finished_up = finish(turned_up, self.z, moments[5], self.main)
        finished = finished_gate, finished_up, finished_down
        edges = jnp.zeros((self.owners, 3, HALF, HALF), jnp.float32)
        edges = lax.dynamic_update_slice_in_dim(
            edges, jnp.concatenate([v[2] for v in finished]), 0, 0
        )
        kept_rest, sent_rest = self.halves(edges)
        received_rest = shift(sent_rest, "x", 1)
        last_factor = newton([kept_last, received_last])
        main_line = self.along_sent(main_factors)
        gains = gains + shift(gains, "c", 1)
        attn_arrived, received_rest, last_factor, main_line, gains = lax.optimization_barrier(
            (attn_arrived, received_rest, last_factor, main_line, gains)
        )

        rest_arrived = self.arrive(self.send((kept_rest + received_rest)[:, None]))
        main_line = self.in_order(main_line)
        main_across = shift(main_line, "x", 1)
        factors = jnp.concatenate([last_factor, newton(attn_arrived)])
        gains = gains + shift(gains, "y", 1)
        rest_arrived, main_across, factors, gains = lax.optimization_barrier(
            (rest_arrived, main_across, factors, gains)
        )

        grads += [v[0] for v in finished]
        states += [v[1] for v in finished]
        line = self.along_sent(factors)
        rest_factors = newton(rest_arrived)
        gains = gains + shift(gains, "x", 1)
        line, rest_factors, gains = lax.optimization_barrier((line, rest_factors, gains))

        line = self.in_order(line)
        across = shift(line, "x", 1)
        rest_line = self.along_sent(rest_factors)
        main = self.main_blocks(main_line, main_across)
        across, rest_line = lax.optimization_barrier((across, rest_line))

        gains = gains + sum(shift(gains, "z", k) for k in range(1, self.depth))
        rest_line = self.in_order(rest_line)
        rest = self.both(rest_line, shift(rest_line, "x", 1))
        rest = rest.reshape((-1,) + rest.shape[3:])
        main = jnp.concatenate([main, self.main_blocks(line[:, :1], across[:, :1])])
        attn_factors = self.both(line[:, 1], across[:, 1])
        attn_factors = attn_factors.reshape((-1,) + attn_factors.shape[2:])
        counts, starts = spans(states[:4])
        updates = [apply_factor(v, attn_factors, s) for v, s in zip(states[:4], starts)]
        for i, order in enumerate((1, 2, 0)):
            blocks = main.shape[1]
            partly = apply_factor(states[4 + i], main[order], 0, 0, blocks)
            updates.append(apply_factor(states[4 + i], rest, i, blocks, blocks + 1, partly))
        return grads, states, updates, input_grad, gains

    def along_sent(self, values):
        return [values] + [shift(values, "z", k) for k in range(1, self.depth)]

    def in_order(self, arrived):
        line = jnp.zeros((self.depth,) + arrived[0].shape, arrived[0].dtype)
        for k, values in enumerate(arrived):
            line = place(line, values, self.back(k))
        return line

    def main_blocks(self, line, across):
        full = self.both(line, across)
        full = full.transpose(2, 1, 0, 3, 4, 5)
        return full.reshape(full.shape[:1] + (-1,) + full.shape[3:])

    def both(self, line, across):
        full = jnp.zeros((2,) + line.shape, line.dtype)
        return place(place(full, line, self.x), across, 1 - self.x)


def muon(ways, states):
    counts, starts = spans(states)
    slots = -(-sum(counts) // ways.owners) * ways.owners
    factors = ways.factor_gather(newton(ways.gram_sum(grams(states, slots))))
    return [apply_factor(state, factors, start) for state, start in zip(states, starts)]


def shards(
    ways,
    tokens,
    cotangent,
    dealt_lengths,
    norm_gains,
    query_weight,
    key_matrix,
    value_matrix,
    out_weight,
    gate_weight,
    up_weight,
    down_weight,
    moment_query,
    moment_key,
    moment_value,
    moment_out,
    moment_gate,
    moment_up,
    moment_down,
):
    ways.setup()
    local_rows = tokens.shape[0]
    segment, position, is_alive = slot_layout(dealt_lengths[0])
    rotary_cosines, rotary_sines = rope_tables(position)
    my_alive = lax.dynamic_slice_in_dim(is_alive, ways.part * local_rows, local_rows)
    query_cols = query_weight.shape[1]
    kv_cols = key_matrix.shape[1]
    kv_heads = kv_cols // HEAD_SIZE
    group_width = QUERY_HEADS // KEY_VALUE_HEADS
    cuts = (query_cols, query_cols + kv_cols)

    norm_gains = ways.features_in(norm_gains)
    inputs = ways.features_in(tokens).astype(jnp.float32)
    normalized_input, inverse_in = norm_forward(inputs, norm_gains[0])
    normed_full, mixed_full, out_full, gate_full = ways.open(
        normalized_input.astype(jnp.bfloat16),
        jnp.concatenate([query_weight, key_matrix, value_matrix], axis=1),
        out_weight,
        gate_weight,
        up_weight,
        down_weight,
        (moment_down, moment_gate, moment_up),
    )
    projected = jnp.dot(normed_full, mixed_full, preferred_element_type=jnp.float32)
    alive_flags = is_alive.astype(jnp.int32)
    marks = (segment[:, None], segment[None, :], alive_flags[:, None], alive_flags[None, :])
    heads = query_cols // HEAD_SIZE
    square = jax.ShapeDtypeStruct((heads, GROUP_SLOTS, GROUP_SLOTS), jnp.float32)
    narrow_rows = [
        jax.ShapeDtypeStruct((GROUP_SLOTS, c), jnp.bfloat16)
        for c in (query_cols, kv_cols, kv_cols, query_cols)
    ]
    *kept_attention, mixed_heads = whole_call(
        partial(attend_body, kv_heads, group_width),
        [*narrow_rows[:3], square, square, narrow_rows[3]],
        projected,
        rotary_cosines,
        rotary_sines,
        *marks,
    )
    partial_attended, up_full = ways.beside_attention(contract_last(mixed_heads, out_full))
    attended = ways.beside_sum(partial_attended)
    normed_attn, inverse_attn = norm_forward(attended, norm_gains[1])
    middle = inputs + normed_attn
    normed_mid, inverse_mid = norm_forward(middle, norm_gains[2])
    mid_full = ways.beside_rows(normed_mid.astype(jnp.bfloat16))
    hidden, activated, pulled = enter(mid_full, gate_full, up_full)
    hidden, down_full = ways.beside_hidden(hidden)
    feed_out, _ = ways.mlp_sum([hidden], [down_full])
    normed_feed, inverse_feed = norm_forward(feed_out, norm_gains[3])
    block_output = (middle + normed_feed).astype(jnp.bfloat16)

    upstream = jnp.where(my_alive[:, None], ways.features_in(cotangent).astype(jnp.float32), 0.0)
    delta_feed, gain_feed = norm_backward(feed_out, inverse_feed, norm_gains[3], upstream)
    feed_grad = ways.mlp_rows(delta_feed.astype(jnp.bfloat16))
    partial_down = outer(feed_grad, hidden)
    total_down = ways.mlp_sum_rows(partial_down)
    feed_grad = after(feed_grad, partial_down)
    delta_gate, delta_up = leave(feed_grad, down_full, activated, pulled)
    delta_mid, token = ways.mlp_sum([delta_gate, delta_up], [gate_full, up_full])
    total_gate = ways.mlp_sum_rows(outer(after(mid_full, token), delta_gate))

    mid_back, gain_mid = norm_backward(middle, inverse_mid, norm_gains[2], delta_mid)
    delta_middle = upstream + mid_back
    delta_attended, gain_attn = norm_backward(attended, inverse_attn, norm_gains[1], delta_middle)
    attn_grad = ways.attn_rows_beside(delta_attended.astype(jnp.bfloat16))
    total_up = ways.mlp_sum_rows(outer(after(mid_full, attn_grad), delta_up))
    partial_out = narrow(contract_first(attn_grad, mixed_heads))

    def attention_backward(start):
        delta_mixed = narrow(product(after(attn_grad, start), out_full))
        delta_mixed_proj = whole_call(
            partial(attend_back_body, kv_heads, group_width),
            jax.ShapeDtypeStruct((GROUP_SLOTS, query_cols + 2 * kv_cols), jnp.bfloat16),
            delta_mixed,
            rotary_cosines,
            rotary_sines,
            *marks,
            *kept_attention,
        )
        partial_mixed = narrow(contract_first(normed_full, delta_mixed_proj))
        return partial_mixed, contract_last(delta_mixed_proj, mixed_full)

    moments = (
        moment_query,
        moment_key,
        moment_value,
        moment_out,
        moment_gate,
        moment_up,
        moment_down,
    )
    def end_norm(delta_normed):
        in_back, gain_in = norm_backward(inputs, inverse_in, norm_gains[0], delta_normed)
        gains = jnp.stack([gain_in, gain_attn, gain_mid, gain_feed])
        return delta_middle + in_back, gains

    grads, states, updates, input_grad, gain_grads = ways.close(
        partial_out, attention_backward, (total_down, total_gate, total_up), moments, end_norm
    )
    return (
        ways.features_out(block_output),
        ways.features_out(input_grad),
        ways.features_out(gain_grads),
        *grads,
        *states,
        *updates,
    )


def solution(mesh):
    sizes = dict(mesh.shape)
    if sizes == {"dp": 8, "tensor": 4}:
        mesh = Mesh(mesh.devices.reshape(4, 2, 2, 2), ("z", "x", "y", "c"))
        ways = Grid(dict(mesh.shape))
    else:
        ways = Plain(sizes)
    token_spec, weight_spec = ways.token_spec, ways.weight_spec
    return jax.shard_map(
        partial(shards, ways),
        mesh=mesh,
        in_specs=(token_spec, token_spec, ways.length_spec, P()) + (weight_spec,) * 14,
        out_specs=(token_spec, token_spec, P()) + (weight_spec,) * 21,
        check_vma=False,
    )
```

```python
from functools import partial

import jax
import jax.numpy as jnp
from jax import lax
from jax.experimental import pallas as pl
from jax.experimental.pallas import tpu as pltpu
from jax.sharding import Mesh
from jax.sharding import PartitionSpec as P

MODEL_WIDTH = 2304
QUERY_HEADS = 8
KEY_VALUE_HEADS = 4
HEAD_SIZE = 256
WINDOW = 4096
BLK = 128
NS_STEPS = 5
GROUP_BLOCKS = 4
GROUP_SLOTS = 512


epsilon = 1e-06
softcap = 50.0
rope_base = 10000.0
coef_first = 3.4445
coef_second = -4.775
coef_third = 2.0315
momentum_decay = 0.95
learn_rate = 0.2
masked_value = -1e30


def slot_layout(lengths):
    blocks = (lengths + BLK - 1) // BLK
    block_ends = jnp.cumsum(blocks, dtype=jnp.int32) * BLK
    slot_index = jnp.arange(GROUP_SLOTS, dtype=jnp.int32)
    passed = slot_index[:, None] >= block_ends[None, :]
    segment = jnp.sum(passed.astype(jnp.int32), axis=1, dtype=jnp.int32)
    before = jnp.sum(jnp.where(passed, blocks[None, :] * BLK, 0), axis=1, dtype=jnp.int32)
    position = slot_index - before
    in_segment = segment[:, None] == jnp.arange(GROUP_BLOCKS, dtype=jnp.int32)[None, :]
    own_length = jnp.sum(jnp.where(in_segment, lengths[None, :], 0), axis=1, dtype=jnp.int32)
    is_alive = position < own_length
    return (segment, position, is_alive)


def allowed_pairs(segment, is_alive):
    slot_index = jnp.arange(GROUP_SLOTS, dtype=jnp.int32)
    distance = slot_index[:, None] - slot_index[None, :]
    same_segment = segment[:, None] == segment[None, :]
    inside = (
        is_alive[:, None] & is_alive[None, :] & same_segment & (distance >= 0) & (distance < WINDOW)
    )
    return (distance == 0) | inside


def rope_tables(position):
    half_width = HEAD_SIZE // 2
    frequency = rope_base ** (-2.0 * jnp.arange(half_width, dtype=jnp.float32) / HEAD_SIZE)
    angles = position.astype(jnp.float32)[:, None] * frequency[None, :]
    return (jnp.cos(angles), jnp.sin(angles))


def apply_rotary(values, rotary_cosines, rotary_sines):
    half_width = HEAD_SIZE // 2
    first_half = values[..., :half_width]
    second_half = values[..., half_width:]
    rotary_cosines = rotary_cosines[:, None, :]
    rotary_sines = rotary_sines[:, None, :]
    return jnp.concatenate(
        [
            first_half * rotary_cosines - second_half * rotary_sines,
            second_half * rotary_cosines + first_half * rotary_sines,
        ],
        axis=-1,
    )


def norm_forward(values, gain):
    inverse = lax.rsqrt(jnp.mean(values * values, axis=-1, keepdims=True) + epsilon)
    return (values * inverse * gain, inverse)


def norm_backward(values, inverse, gain, upstream):
    scaled = upstream * gain
    row_inner = jnp.mean(scaled * values, axis=-1, keepdims=True)
    return (
        inverse * scaled - values * inverse**3 * row_inner,
        jnp.sum(upstream * values * inverse, axis=0),
    )


def contract_last(left_side, right_side):
    return lax.dot_general(
        left_side, right_side, (((1,), (1,)), ((), ())), preferred_element_type=jnp.float32
    )


def contract_first(left_side, right_side):
    return lax.dot_general(
        left_side, right_side, (((0,), (0,)), ((), ())), preferred_element_type=jnp.float32
    )


HALF = HEAD_SIZE // 2

BRIEF = pl.CostEstimate(flops=1024, bytes_accessed=1024, transcendentals=0)


def two_terms(values):
    high = values.astype(jnp.bfloat16)
    low = (values - high.astype(jnp.float32)).astype(jnp.bfloat16)
    return high, low


def product(left_side, right_side):
    return jnp.dot(left_side, right_side, preferred_element_type=jnp.float32)


def product_f32(left_terms, right_terms):
    left_high, left_low = left_terms
    right_high, right_low = right_terms
    return product(left_high, right_high) + (
        product(left_high, right_low) + product(left_low, right_high)
    )


def gram_body(counts, *refs):
    out_ref = refs[-1]
    step = pl.program_id(0)
    start = 0
    for ref, count in zip(refs[:-1], counts):

        @pl.when((step >= start) & (step < start + count))
        def _(ref=ref):
            high, low = two_terms(ref[...])
            mixed = contract_first(high, low)
            gram = contract_first(high, high) + (mixed + mixed.T)
            out_ref[0, 0] = gram[:HALF, :HALF]
            out_ref[0, 1] = gram[:HALF, HALF:]
            out_ref[0, 2] = gram[HALF:, HALF:]

        start += count

    @pl.when(step >= start)
    def _():
        out_ref[...] = jnp.zeros(out_ref.shape, out_ref.dtype)


def clamped(start, count):
    return lambda step: (0, jnp.clip(step - start, 0, count - 1))


def spans(states):
    counts = [state.shape[1] // HEAD_SIZE for state in states]
    starts = [sum(counts[:i]) for i in range(len(counts))]
    return counts, starts


def grams(states, slots):
    counts, starts = spans(states)
    rows = states[0].shape[0]
    return pl.pallas_call(
        partial(gram_body, counts),
        grid=(slots,),
        in_specs=[
            pl.BlockSpec((rows, HEAD_SIZE), clamped(s, c)) for s, c in zip(starts, counts)
        ],
        out_specs=pl.BlockSpec((1, 3, HALF, HALF), lambda step: (step, 0, 0, 0)),
        out_shape=jax.ShapeDtypeStruct((slots, 3, HALF, HALF), jnp.float32),
        cost_estimate=BRIEF,
        compiler_params=pltpu.CompilerParams(vmem_limit_bytes=40 * 1024 * 1024),
    )(*states)


def add_gram(out_ref, index, values):
    high, low = two_terms(values)
    mixed = contract_first(high, low)
    gram = contract_first(high, high) + (mixed + mixed.T)
    out_ref[index, 0] += gram[:HALF, :HALF]
    out_ref[index, 1] += gram[:HALF, HALF:]
    out_ref[index, 2] += gram[HALF:, HALF:]


def inner_body(total_ref, moment_ref, out_ref):
    out_ref[...] = jnp.zeros(out_ref.shape, out_ref.dtype)
    gradient = total_ref[...].astype(jnp.float32)
    add_gram(out_ref, 0, momentum_decay * moment_ref[...].astype(jnp.float32) + gradient)


def inner_grams(total, moment, blocks, first):
    rows = total.shape[0]
    return pl.pallas_call(
        inner_body,
        grid=(blocks,),
        in_specs=[
            pl.BlockSpec((rows, HEAD_SIZE), lambda step: (0, step)),
            pl.BlockSpec((rows, HEAD_SIZE), lambda step: (0, step + first)),
        ],
        out_specs=pl.BlockSpec((1, 3, HALF, HALF), lambda step: (step, 0, 0, 0)),
        out_shape=jax.ShapeDtypeStruct((blocks, 3, HALF, HALF), jnp.float32),
        cost_estimate=BRIEF,
        compiler_params=pltpu.CompilerParams(vmem_limit_bytes=40 * 1024 * 1024),
    )(total, moment)


ROW_TILE = 96


def finish_body(main, place_ref, *refs):
    depth = len(refs) - 4
    moment_ref, grad_ref, state_ref, gram_ref = refs[depth:]
    rest = refs[0].shape[1] - main
    for j in range(depth):
        turn = lax.rem(place_ref[0] + depth - j, depth)
        for k in range(depth):

            @pl.when(turn == k)
            def _(piece=refs[k], j=j):
                grad_ref[:, main * j : main * (j + 1)] = piece[:, :main].astype(jnp.float32)
                start = main * depth + rest * j
                grad_ref[:, start : start + rest] = piece[:, main:].astype(jnp.float32)

    state_ref[...] = momentum_decay * moment_ref[...] + grad_ref[...]

    @pl.when(pl.program_id(0) == 0)
    def _():
        gram_ref[...] = jnp.zeros(gram_ref.shape, gram_ref.dtype)

    add_gram(gram_ref, 0, state_ref[:, main * depth :])


def finish(pieces, position, moment, main):
    rows, cols = moment.shape
    wide_spec = pl.BlockSpec((ROW_TILE, cols), lambda step, place: (step, 0))
    piece_spec = pl.BlockSpec((ROW_TILE, pieces[0].shape[1]), lambda step, place: (step, 0))
    return pl.pallas_call(
        partial(finish_body, main),
        grid_spec=pltpu.PrefetchScalarGridSpec(
            num_scalar_prefetch=1,
            grid=(rows // ROW_TILE,),
            in_specs=[piece_spec] * len(pieces) + [wide_spec],
            out_specs=[
                wide_spec,
                wide_spec,
                pl.BlockSpec((1, 3, HALF, HALF), lambda step, place: (0, 0, 0, 0)),
            ],
        ),
        out_shape=[
            jax.ShapeDtypeStruct((rows, cols), jnp.float32),
            jax.ShapeDtypeStruct((rows, cols), jnp.float32),
            jax.ShapeDtypeStruct((1, 3, HALF, HALF), jnp.float32),
        ],
        cost_estimate=BRIEF,
        compiler_params=pltpu.CompilerParams(vmem_limit_bytes=40 * 1024 * 1024),
    )(position.reshape(1), *pieces, moment)


def attn_finish_body(depth, *refs):
    sums = refs[: 2 * depth]
    moments, grads, states = (refs[2 * depth + 4 * i : 2 * depth + 4 * i + 4] for i in range(3))
    gram_ref = refs[-1]

    @pl.when(pl.program_id(0) == 0)
    def _():
        gram_ref[...] = jnp.zeros(gram_ref.shape, gram_ref.dtype)

    mixed = sum(ref[...].astype(jnp.float32) for ref in sums[:depth])
    out = sum(ref[...].astype(jnp.float32) for ref in sums[depth:])
    slot = 0
    start = 0
    for moment_ref, grad_ref, state_ref in zip(moments, grads, states):
        cols = moment_ref.shape[1]
        if grad_ref is grads[-1]:
            gradient = out
        else:
            gradient = mixed[:, start : start + cols]
        start += cols
        grad_ref[...] = gradient
        state = momentum_decay * moment_ref[...] + gradient
        state_ref[...] = state
        for block in range(cols // HEAD_SIZE):
            add_gram(gram_ref, slot, state[:, block * HEAD_SIZE : (block + 1) * HEAD_SIZE])
            slot += 1


def attn_finish(mixed, out, moments, slots):
    rows = moments[0].shape[0]

    def spec(v):
        return pl.BlockSpec((ROW_TILE, v.shape[1]), lambda step: (step, 0))

    outs = [jax.ShapeDtypeStruct(m.shape, jnp.float32) for m in moments]
    results = pl.pallas_call(
        partial(attn_finish_body, len(mixed)),
        grid=(rows // ROW_TILE,),
        in_specs=[spec(v) for v in (*mixed, *out, *moments)],
        out_specs=[spec(v) for v in outs + outs]
        + [pl.BlockSpec((slots, 3, HALF, HALF), lambda step: (0, 0, 0, 0))],
        out_shape=outs + outs + [jax.ShapeDtypeStruct((slots, 3, HALF, HALF), jnp.float32)],
        cost_estimate=BRIEF,
        compiler_params=pltpu.CompilerParams(vmem_limit_bytes=40 * 1024 * 1024),
    )(*mixed, *out, *moments)
    return list(results[:4]), list(results[4:8]), results[8]


def newton_body(count, *refs):
    out_ref = refs[-1]
    row = lax.broadcasted_iota(jnp.int32, (HEAD_SIZE, HEAD_SIZE), 0)
    col = lax.broadcasted_iota(jnp.int32, (HEAD_SIZE, HEAD_SIZE), 1)
    unit = (row == col).astype(jnp.float32)
    squares = []
    scales = []
    for i in range(count):
        parts = [sum(ref[i, j].astype(jnp.float32) for ref in refs[:-1]) for j in range(3)]
        gram = jnp.concatenate(
            [
                jnp.concatenate([parts[0], parts[1]], axis=1),
                jnp.concatenate([parts[1].T, parts[2]], axis=1),
            ],
            axis=0,
        )
        total = jnp.sum(jnp.sum(gram * unit, axis=1, keepdims=True), axis=0, keepdims=True)
        inverse = 1.0 / (jnp.sqrt(total) + 1e-07)
        squares.append(gram * inverse * inverse)
        scales.append(-learn_rate * (MODEL_WIDTH / HEAD_SIZE) ** 0.5 * inverse)
    totals = [None] * count
    for repeat in range(NS_STEPS):
        terms = [two_terms(square) for square in squares]
        seconds = [product_f32(t, t) for t in terms]
        steps = [
            coef_first * unit + (coef_second * square + coef_third * second)
            for square, second in zip(squares, seconds)
        ]
        step_terms = [two_terms(step) for step in steps]
        if repeat == 0:
            totals = steps
        else:
            totals = [
                product_f32(two_terms(total), s) for total, s in zip(totals, step_terms)
            ]
        if repeat < NS_STEPS - 1:
            inner = [product_f32(s, t) for s, t in zip(step_terms, terms)]
            squares = [product_f32(two_terms(v), s) for v, s in zip(inner, step_terms)]
    for i in range(count):
        result = (totals[i] * scales[i]).astype(out_ref.dtype)
        out_ref[i, 0] = result[:HALF, :HALF]
        out_ref[i, 1] = result[:HALF, HALF:]
        out_ref[i, 2] = result[HALF:, HALF:]


def newton(pieces):
    count = pieces[0].shape[0]
    return pl.pallas_call(
        partial(newton_body, count),
        out_shape=jax.ShapeDtypeStruct((count, 3, HALF, HALF), jnp.bfloat16),
        cost_estimate=BRIEF,
        compiler_params=pltpu.CompilerParams(vmem_limit_bytes=40 * 1024 * 1024),
    )(*pieces)


def apply_body(state_ref, factor_ref, *refs):
    out_ref = refs[-1]
    upper = factor_ref[0, 1].astype(jnp.float32)
    factor = jnp.concatenate(
        [
            jnp.concatenate([factor_ref[0, 0], factor_ref[0, 1]], axis=1),
            jnp.concatenate([upper.T.astype(jnp.bfloat16), factor_ref[0, 2]], axis=1),
        ],
        axis=0,
    )
    high, low = two_terms(state_ref[...])
    out_ref[...] = product(high, factor) + product(low, factor)


def apply_factor(state, factors, start, low=0, high=None, into=None):
    rows, cols = state.shape
    high = cols // HEAD_SIZE if high is None else high
    block = pl.BlockSpec((rows, HEAD_SIZE), lambda step: (0, step + low))
    return pl.pallas_call(
        apply_body,
        grid=(high - low,),
        in_specs=[block, pl.BlockSpec((1, 3, HALF, HALF), lambda step: (step + start, 0, 0, 0))]
        + ([] if into is None else [pl.BlockSpec(memory_space=pl.ANY)]),
        out_specs=block,
        out_shape=jax.ShapeDtypeStruct((rows, cols), jnp.float32),
        input_output_aliases={} if into is None else {2: 0},
        cost_estimate=BRIEF,
        compiler_params=pltpu.CompilerParams(vmem_limit_bytes=40 * 1024 * 1024),
    )(state, factors, *([] if into is None else [into]))


VMEM_BYTES = 50 * 1024 * 1024


def dense_call(body, grid, in_specs, out_specs, out_shape, *operands):
    return pl.pallas_call(
        body,
        grid=grid,
        in_specs=in_specs,
        out_specs=out_specs,
        out_shape=out_shape,
        cost_estimate=BRIEF,
        compiler_params=pltpu.CompilerParams(vmem_limit_bytes=VMEM_BYTES),
    )(*operands)


def column_tile(width):
    return width if width % 768 else 768


def enter_body(rows_ref, gate_ref, up_ref, hidden_ref, gelu_ref, pull_ref):
    rows = rows_ref[...]
    factor = (2.0 / jnp.pi) ** 0.5
    for p in range(gate_ref.shape[0]):
        gate = product(rows, gate_ref[p])
        up = product(rows, up_ref[p])
        squared = gate * gate
        bend = jnp.tanh(factor * (gate + 0.044715 * gate * squared))
        upper = 0.5 * (1.0 + bend)
        gelu = gate * upper
        slope = upper + 0.5 * gate * (1.0 - bend * bend) * (factor * (1.0 + 0.134145 * squared))
        hidden_ref[p] = (gelu * up).astype(jnp.bfloat16)
        gelu_ref[p] = gelu.astype(jnp.bfloat16)
        pull_ref[p] = (up * slope).astype(jnp.bfloat16)


def enter(rows, gate, up):
    count, width = rows.shape
    pieces, _, cols = gate.shape
    tile = column_tile(cols)
    weight = pl.BlockSpec((pieces, width, tile), lambda j, i: (0, 0, j))
    out = pl.BlockSpec((pieces, 256, tile), lambda j, i: (0, i, j))
    return dense_call(
        enter_body,
        (cols // tile, count // 256),
        [pl.BlockSpec((256, width), lambda j, i: (i, 0)), weight, weight],
        [out] * 3,
        [jax.ShapeDtypeStruct((pieces, count, cols), jnp.bfloat16)] * 3,
        rows,
        gate,
        up,
    )


def leave_body(rows_ref, down_ref, gelu_ref, pull_ref, gate_ref, up_ref):
    rows = rows_ref[...]
    for p in range(down_ref.shape[0]):
        delta = product(rows, down_ref[p])
        gate_ref[p] = (delta * pull_ref[p].astype(jnp.float32)).astype(jnp.bfloat16)
        up_ref[p] = (delta * gelu_ref[p].astype(jnp.float32)).astype(jnp.bfloat16)


def leave(rows, down, gelu, pull):
    count, width = rows.shape
    pieces, _, cols = down.shape
    tile = column_tile(cols)
    out = pl.BlockSpec((pieces, 256, tile), lambda j, i: (0, i, j))
    return dense_call(
        leave_body,
        (cols // tile, count // 256),
        [
            pl.BlockSpec((256, width), lambda j, i: (i, 0)),
            pl.BlockSpec((pieces, width, tile), lambda j, i: (0, 0, j)),
            out,
            out,
        ],
        [out] * 2,
        [jax.ShapeDtypeStruct((pieces, count, cols), jnp.bfloat16)] * 2,
        rows,
        down,
        gelu,
        pull,
    )


def shrink_body(count, *refs):
    pieces = refs[0].shape[0]
    total = None
    for i in range(count):
        for p in range(pieces):
            term = contract_last(refs[i][p], refs[count + i][p])
            total = term if total is None else total + term
    refs[-1][...] = total.astype(refs[-1].dtype)


def shrink(lefts, rights, rows, part, dtype):
    pieces, width, cols = rights[0].shape
    count = len(lefts)
    tile = 768 if cols < 768 else 256
    return dense_call(
        partial(shrink_body, count),
        (width // tile,),
        [pl.BlockSpec((pieces, rows, cols), lambda j: (0, part, 0))] * count
        + [pl.BlockSpec((pieces, tile, cols), lambda j: (0, j, 0))] * count,
        pl.BlockSpec((rows, tile), lambda j: (0, j)),
        jax.ShapeDtypeStruct((rows, width), dtype),
        *lefts,
        *rights,
    )


def outer_body(left_ref, right_ref, out_ref):
    left = left_ref[...]
    for p in range(out_ref.shape[0]):
        out_ref[p] = contract_first(left, right_ref[p]).astype(jnp.bfloat16)


def outer(left, right):
    rows, width = left.shape
    pieces, _, cols = right.shape
    tile = 384 if cols < 768 else 256
    return dense_call(
        outer_body,
        (width // tile,),
        [
            pl.BlockSpec((rows, tile), lambda j: (0, j)),
            pl.BlockSpec((pieces, rows, cols), lambda j: (0, 0, 0)),
        ],
        pl.BlockSpec((pieces, tile, cols), lambda j: (0, j, 0)),
        jax.ShapeDtypeStruct((pieces, width, cols), jnp.bfloat16),
        left,
        right,
    )


def rotated(values, cosines, sines):
    first, second = values[:, :HALF], values[:, HALF:]
    return jnp.concatenate(
        [first * cosines - second * sines, second * cosines + first * sines], axis=1
    )


def head(index):
    return slice(index * HEAD_SIZE, (index + 1) * HEAD_SIZE)


def pair_mask(segment_rows, segment_cols, alive_rows, alive_cols):
    shape = (segment_rows.shape[0], segment_cols.shape[1])
    distance = lax.broadcasted_iota(jnp.int32, shape, 0) - lax.broadcasted_iota(
        jnp.int32, shape, 1
    )
    inside = (
        (alive_rows * alive_cols > 0)
        & (segment_rows == segment_cols)
        & (distance >= 0)
        & (distance < WINDOW)
    )
    return (distance == 0) | inside


def attend_body(kv_heads, width, *refs):
    projected, cosines, sines = (ref[...] for ref in refs[:3])
    query_ref, key_ref, value_ref, prob_ref, tanh_ref, mixed_ref = refs[7:]
    allowed = pair_mask(*(ref[...] for ref in refs[3:7]))
    query_heads = kv_heads * width
    for j in range(kv_heads):
        key = rotated(projected[:, head(query_heads + j)], cosines, sines).astype(jnp.bfloat16)
        value = projected[:, head(query_heads + kv_heads + j)].astype(jnp.bfloat16)
        key_ref[:, head(j)] = key
        value_ref[:, head(j)] = value
        for i in range(j * width, (j + 1) * width):
            query = rotated(projected[:, head(i)], cosines, sines) * HEAD_SIZE ** (-0.5)
            query = query.astype(jnp.bfloat16)
            query_ref[:, head(i)] = query
            tanh_part = jnp.tanh(contract_last(query, key) / softcap)
            masked = jnp.where(allowed, softcap * tanh_part, masked_value)
            exponent = jnp.exp(masked - jnp.max(masked, axis=-1, keepdims=True))
            prob = exponent / jnp.sum(exponent, axis=-1, keepdims=True)
            prob_ref[i] = prob
            tanh_ref[i] = tanh_part
            mixed_ref[:, head(i)] = product(prob.astype(jnp.bfloat16), value).astype(jnp.bfloat16)


def attend_back_body(kv_heads, width, *refs):
    delta_mixed, cosines, sines = (ref[...] for ref in refs[:3])
    query_ref, key_ref, value_ref, prob_ref, tanh_ref, out_ref = refs[7:]
    allowed = pair_mask(*(ref[...] for ref in refs[3:7]))
    query_heads = kv_heads * width
    for j in range(kv_heads):
        key, value = key_ref[:, head(j)], value_ref[:, head(j)]
        delta_key = delta_value = None
        for i in range(j * width, (j + 1) * width):
            delta = delta_mixed[:, head(i)]
            prob, tanh_part = prob_ref[i], tanh_ref[i]
            delta_prob = contract_last(delta, value)
            inner = jnp.sum(prob * delta_prob, axis=-1, keepdims=True)
            raw = jnp.where(allowed, prob * (delta_prob - inner), 0.0)
            raw = (raw * (1.0 - tanh_part * tanh_part)).astype(jnp.bfloat16)
            delta_query = product(raw, key) * HEAD_SIZE ** (-0.5)
            out_ref[:, head(i)] = rotated(delta_query, cosines, -sines).astype(jnp.bfloat16)
            key_term = contract_first(raw, query_ref[:, head(i)])
            value_term = contract_first(prob.astype(jnp.bfloat16), delta)
            delta_key = key_term if delta_key is None else delta_key + key_term
            delta_value = value_term if delta_value is None else delta_value + value_term
        out_ref[:, head(query_heads + j)] = rotated(delta_key, cosines, -sines).astype(
            jnp.bfloat16
        )
        out_ref[:, head(query_heads + kv_heads + j)] = delta_value.astype(jnp.bfloat16)


def whole_call(body, out_shape, *operands):
    return pl.pallas_call(
        body,
        out_shape=out_shape,
        cost_estimate=BRIEF,
        compiler_params=pltpu.CompilerParams(vmem_limit_bytes=VMEM_BYTES),
    )(*operands)


def join_body(*refs):
    start = 0
    for ref in refs[:-1]:
        refs[-1][:, start : start + ref.shape[1]] = ref[...]
        start += ref.shape[1]


def joined(pieces):
    shape = (pieces[0].shape[0], sum(v.shape[1] for v in pieces))
    return whole_call(join_body, jax.ShapeDtypeStruct(shape, pieces[0].dtype), *pieces)


def fence(*values):
    return lax.optimization_barrier(values)


def after(value, *others):
    return lax.optimization_barrier((value,) + others)[0]


class Plain:
    def __init__(self, sizes):
        self.owners = sizes["dp"]
        self.token_spec = P(("dp", "tensor"), None)
        self.length_spec = P("dp", None)
        self.weight_spec = P("dp", "tensor")
        self.every = ("dp", "tensor")

    def setup(self):
        self.part = lax.axis_index("tensor")

    def gather_dp(self, shard):
        return lax.all_gather(shard, "dp", axis=0, tiled=True)

    def scatter_dp(self, partial_sum):
        return wide(lax.psum_scatter(partial_sum, "dp", scatter_dimension=0, tiled=True))

    def open(self, normed, mixed, out, gate, up, down, moments):
        self.later = {"up": up, "down": down}
        return (
            self.attn_rows(normed),
            self.gather_dp(jnp.concatenate(mixed, axis=1)),
            self.gather_dp(out),
            self.gather_dp(gate)[None],
        )

    def beside_attention(self, values):
        return values, self.gather_dp(self.later["up"])[None]

    def beside_sum(self, values):
        return self.attn_sum(values)

    def beside_rows(self, values):
        return self.attn_rows(values)

    def beside_hidden(self, values):
        return values, self.gather_dp(self.later["down"])[None]

    def attn_rows(self, values):
        return lax.all_gather(values, "tensor", axis=0, tiled=True)

    def attn_sum(self, values):
        return lax.psum_scatter(values, "tensor", scatter_dimension=0, tiled=True)

    def features_in(self, values):
        return values

    def features_out(self, values):
        return values

    def mlp_sum_rows(self, partial_sums):
        return self.scatter_dp(partial_sums[0])

    def close(self, partial_out, attention_backward, totals, moments, end_norm):
        partial_mixed, partial_normed = attention_backward(partial_out)
        cuts = (moments[0].shape[1], moments[0].shape[1] + moments[1].shape[1])
        grads = jnp.split(self.scatter_dp(partial_mixed), cuts, axis=1)
        grads = (*grads, self.scatter_dp(partial_out), totals[1], totals[2], totals[0])
        states = [momentum_decay * m + g for m, g in zip(moments, grads)]
        first = muon(self, states[6:] + states[4:5])
        last = muon(self, states[5:6] + states[:4])
        updates = (*last[1:], first[1], last[0], first[0])
        input_grad, gains = end_norm(self.attn_sum(partial_normed))
        return grads, states, updates, input_grad, self.sum_every(gains)

    def sum_every(self, values):
        return lax.psum(values, self.every)

    def mlp_rows(self, values):
        return self.attn_rows(values)

    def mlp_sum(self, lefts, rights):
        values = shrink(lefts, rights, lefts[0].shape[1], 0, jnp.float32)
        return self.attn_sum(values), values

    def attn_rows_beside(self, values):
        return self.attn_rows(values)

    def gram_sum(self, values):
        return [lax.psum_scatter(values, "dp", scatter_dimension=0, tiled=True)]

    def factor_gather(self, values):
        return lax.all_gather(values, "dp", axis=0, tiled=True)


def shift(values, axis, distance):
    size = lax.axis_size(axis)
    return lax.ppermute(values, axis, [(i, (i + distance) % size) for i in range(size)])


def pick(stacked, index):
    return lax.dynamic_index_in_dim(stacked, index, 0, keepdims=False)


def wide(values):
    return values.astype(jnp.float32)


def narrow(values):
    return values.astype(jnp.bfloat16)


def place(buffer, values, *index):
    fresh = values.reshape((1,) * len(index) + values.shape)
    zero = jnp.zeros((), jnp.int32)
    return lax.dynamic_update_slice(buffer, fresh, tuple(index) + (zero,) * values.ndim)


class Grid:
    def __init__(self, sizes):
        self.depth = sizes["z"]
        self.owners = sizes["z"] * sizes["x"]
        self.token_spec = P(("z", "x", "y", "c"), None)
        self.length_spec = P(("z", "x"), None)
        self.weight_spec = P(("z", "x"), ("y", "c"))
        self.every = ("z", "x", "y", "c")

    def setup(self):
        self.z, self.x, self.y, self.c = (lax.axis_index(a) for a in self.every)
        self.part = self.y * 2 + self.c


    def features_in(self, values):
        split = values.reshape(values.shape[:-1] + (self.depth, 2, -1))
        return jnp.swapaxes(split, -3, -2).reshape(values.shape)

    def features_out(self, values):
        split = values.reshape(values.shape[:-1] + (2, self.depth, -1))
        return jnp.swapaxes(split, -3, -2).reshape(values.shape)

    def back(self, distance):
        return lax.rem(self.z + self.depth - distance, self.depth)

    def ahead(self, distance):
        return lax.rem(self.z + distance, self.depth)

    def open(self, normed, mixed, out, gate, up, down, moments):
        attn = joined((*mixed, out))
        line = [attn, shift(attn, "z", 1)]
        across = [shift(attn, "x", 1)]
        over = shift(normed, "y", 1)
        across[0], line[1], over, gate, up = fence(across[0], line[1], over, gate, up)

        across.append(shift(line[1], "x", 1))
        line.append(shift(line[1], "z", 1))
        pair = shift(jnp.concatenate([normed, over], axis=0), "c", 1)
        gate_sent = self.send(self.quarters(gate))
        across[1], line[2], pair, up, down, *gate_sent = fence(
            across[1], line[2], pair, up, down, *gate_sent
        )

        across.append(shift(line[2], "x", 1))
        line.append(shift(line[2], "z", 1))
        up_sent = self.send(self.quarters(up))
        across[2], line[3], down, gate_sent, up_sent, moments = lax.optimization_barrier(
            (across[2], line[3], down, gate_sent, up_sent, moments)
        )

        across.append(shift(line[3], "x", 1))
        gate_arrived = self.arrive(gate_sent)
        down_sent = self.send(self.quarters(down))
        across[3], gate_arrived, up_sent, down_sent, moments = lax.optimization_barrier(
            (across[3], gate_arrived, up_sent, down_sent, moments)
        )
        self.up_sent, self.down_sent, self.moments = up_sent, down_sent, moments

        mixed_cols = attn.shape[1] - out.shape[1]
        full = jnp.zeros((2, self.depth) + attn.shape, attn.dtype)
        for k in range(self.depth):
            full = place(full, line[k], self.x, self.back(k))
            full = place(full, across[k], 1 - self.x, self.back(k))
        gate_column = self.column(gate_arrived)
        full, gate_column = fence(full.reshape((-1,) + attn.shape[1:]), gate_column)
        return (
            self.order_rows(normed, over, pair),
            full[:, :mixed_cols],
            full[:, mixed_cols:],
            self.gather_plane(gate_column),
        )

    def beside_attention(self, values):
        arrived = self.arrive(self.up_sent)
        values, arrived, down_sent = lax.optimization_barrier((values, arrived, self.down_sent))
        values, column, moments, down_sent = lax.optimization_barrier(
            (values, self.column(arrived), self.moments, down_sent)
        )
        self.down_sent, self.moments = down_sent, moments
        return values, self.gather_plane(column)

    def beside_sum(self, values):
        kept, sent = self.core_half(values)
        received = shift(sent, "c", 1)
        arrived = self.arrive(self.down_sent)
        mine = kept + wide(received)
        total = pick(mine, self.y) + wide(shift(narrow(pick(mine, 1 - self.y)), "y", 1))
        total, arrived = lax.optimization_barrier((total, arrived))
        total, column, moments = lax.optimization_barrier(
            (total, self.column(arrived), self.moments)
        )
        self.down_full = self.gather_plane(column)
        self.moments = moments
        return total

    def beside_rows(self, values):
        values, moments = lax.optimization_barrier((values, self.moments))
        line = [shift(values, "z", k) for k in range(1, self.depth)]
        inner = [self.main_quarters(narrow(m)) for m in moments]
        inner_sent = [
            self.send(jnp.concatenate([inner[0], inner[1]], axis=2)),
            self.send(inner[2]),
        ]
        line, inner_sent = lax.optimization_barrier((line, inner_sent))
        line = jnp.concatenate(line, axis=0)
        pair = shift(values, "c", 1), shift(line, "c", 1)
        values, line, pair, inner_sent = lax.optimization_barrier((values, line, pair, inner_sent))
        self.inner_sent = inner_sent
        return jnp.concatenate([values, line, *pair], axis=0)

    def beside_hidden(self, values):
        arrived = self.arrive(self.inner_sent[0])
        values, arrived = lax.optimization_barrier((values, arrived))
        self.inner = self.column(arrived).reshape(-1, 2 * self.main)
        return values, self.down_full


    def main_quarters(self, shard):
        rows, cols = shard.shape
        self.main = cols // (self.depth * HEAD_SIZE) * HEAD_SIZE
        main = shard[:, : self.depth * self.main]
        return main.reshape(rows, self.depth, self.main).transpose(1, 0, 2)

    def quarters(self, shard):
        main = self.main_quarters(shard)
        rest = shard[:, self.depth * self.main :]
        rest = rest.reshape(shard.shape[0], self.depth, -1).transpose(1, 0, 2)
        return jnp.concatenate([main, rest], axis=2)

    def send(self, chunks):
        return [pick(chunks, self.ahead(k)) for k in range(self.depth)]

    def arrive(self, sent):
        return [sent[0]] + [shift(sent[k], "z", k) for k in range(1, self.depth)]

    def column(self, arrived):
        column = jnp.zeros((self.depth,) + arrived[0].shape, arrived[0].dtype)
        for k, values in enumerate(arrived):
            column = place(column, values, self.back(k))
        return column

    def gather_plane(self, column):
        full = lax.all_gather(column, ("y", "x"), axis=0, tiled=True)
        return full.reshape(2, 2 * self.depth * column.shape[1], -1)

    def order_rows(self, own, over, pair):
        rows = own.shape[0]
        near, far = pair[:rows], pair[rows:]
        first = self.y == 0
        low_own, high_own = jnp.where(first, own, over), jnp.where(first, over, own)
        low_near, high_near = jnp.where(first, near, far), jnp.where(first, far, near)
        core = self.c == 0
        return jnp.concatenate(
            [
                jnp.where(core, low_own, low_near),
                jnp.where(core, low_near, low_own),
                jnp.where(core, high_own, high_near),
                jnp.where(core, high_near, high_own),
            ],
            axis=0,
        )

    def attn_rows(self, values):
        over = shift(values, "y", 1)
        pair = shift(jnp.concatenate([values, over], axis=0), "c", 1)
        return self.order_rows(values, over, pair)

    def core_half(self, values):
        stacked = values.reshape(2, 2, -1, values.shape[1]).transpose(1, 0, 2, 3)
        return pick(stacked, self.c), narrow(pick(stacked, 1 - self.c))

    def attn_sum(self, values):
        kept, sent = self.core_half(values)
        mine = kept + wide(shift(sent, "c", 1))
        return pick(mine, self.y) + wide(shift(narrow(pick(mine, 1 - self.y)), "y", 1))

    def mlp_sum_rows(self, partial_sums):
        stacked = partial_sums.reshape(4 * self.depth, -1, partial_sums.shape[-1])
        return lax.psum_scatter(stacked, ("y", "x"), scatter_dimension=0, tiled=True)

    def mlp_rows(self, values):
        line = jnp.concatenate([shift(values, "z", k) for k in range(1, self.depth)], axis=0)
        return jnp.concatenate([values, line, shift(values, "c", 1), shift(line, "c", 1)], axis=0)

    def mlp_sum(self, lefts, rights):
        rows = lefts[0].shape[1] // 2
        away = shrink(lefts, rights, rows, 1, jnp.bfloat16)
        received = shift(away, "c", 1)
        kept = shrink([after(v, away) for v in lefts], rights, rows, 0, jnp.bfloat16)
        mine = (wide(kept) + wide(received)).reshape(self.depth, -1, kept.shape[1])
        sent = [narrow(mine[k]) for k in range(1, self.depth)]
        own, *sent = fence(mine[0], *sent)
        arrived = [shift(v, "z", self.depth - k) for k, v in enumerate(sent, 1)]
        return own + sum(wide(v) for v in arrived), own

    def attn_rows_beside(self, values):
        values, sent = lax.optimization_barrier((values, self.inner_sent[1]))
        arrived = self.arrive(sent)
        over = shift(values, "y", 1)
        values, over, arrived = lax.optimization_barrier((values, over, arrived))
        self.inner_last = arrived
        pair = shift(jnp.concatenate([values, over], axis=0), "c", 1)
        return self.order_rows(values, over, pair)

    def halves(self, values):
        stacked = values.reshape((2, -1) + values.shape[1:])
        return pick(stacked, self.x), pick(stacked, 1 - self.x)

    def main_grams(self, total, inner, first):
        blocks = self.main // HEAD_SIZE
        rows = total.reshape(-1, total.shape[-1])
        return self.halves(inner_grams(rows, inner, blocks, first * blocks))

    def close(self, partial_out, attention_backward, totals, moments, end_norm):
        total_down, total_gate, total_up = totals

        stacked = partial_out.reshape(2, -1, partial_out.shape[1])
        kept_out, sent_out = pick(stacked, self.x), pick(stacked, 1 - self.x)
        partial_out, sent_out, down_sent = lax.optimization_barrier(
            (partial_out, sent_out, self.send(total_down))
        )
        received = shift(sent_out, "x", 1)
        turned_down = self.arrive(down_sent)
        partial_mixed, partial_normed = attention_backward(partial_out)
        partial_mixed, partial_normed, received, turned_down, total_gate = (
            lax.optimization_barrier(
                (partial_mixed, partial_normed, received, turned_down, total_gate)
            )
        )
        out_rows = (wide(kept_out) + wide(received)).reshape(self.depth, -1, kept_out.shape[1])
        out_sent = self.send(narrow(out_rows))
        gate_sent = self.send(total_gate)
        stacked = partial_mixed.reshape(2, -1, partial_mixed.shape[1])
        kept_mixed, sent_mixed = pick(stacked, self.x), pick(stacked, 1 - self.x)
        kept_normed, sent_normed = self.core_half(partial_normed)
        out_sent, gate_sent, sent_mixed, sent_normed = lax.optimization_barrier(
            (out_sent, gate_sent, sent_mixed, sent_normed)
        )

        received = shift(sent_mixed, "x", 1)
        out_arrived = self.arrive(out_sent)
        turned_gate = self.arrive(gate_sent)
        normed_received = shift(sent_normed, "c", 1)
        kept_down, sent_down = self.main_grams(total_down, self.inner, 0)
        kept_gate, sent_gate = self.main_grams(total_gate, self.inner, 1)
        sent_grams = jnp.concatenate([sent_down, sent_gate])
        received, out_arrived, turned_gate, normed_received, sent_grams, turned_down = (
            lax.optimization_barrier(
                (
                    received,
                    out_arrived,
                    turned_gate,
                    normed_received,
                    sent_grams,
                    turned_down,
                )
            )
        )

        mixed_rows = (wide(kept_mixed) + wide(received)).reshape(
            self.depth, -1, kept_mixed.shape[1]
        )
        mixed_arrived = self.arrive(self.send(narrow(mixed_rows)))
        received_grams = shift(sent_grams, "x", 1)
        mine = kept_normed + wide(normed_received)
        normed_received = shift(narrow(pick(mine, 1 - self.y)), "y", 1)
        finished_down = finish(turned_down, self.z, moments[6], self.main)
        finished_gate = finish(turned_gate, self.z, moments[4], self.main)
        inner_last = self.column(self.inner_last).reshape(-1, self.main)
        mixed_arrived, received_grams, normed_received, inner_last, total_up = (
            lax.optimization_barrier(
                (mixed_arrived, received_grams, normed_received, inner_last, total_up)
            )
        )
        input_grad, gains = end_norm(pick(mine, self.y) + wide(normed_received))

        turned_up = self.arrive(self.send(total_up))
        kept_last, sent_last = self.main_grams(total_up, inner_last, 0)
        received_last = shift(sent_last, "x", 1)
        grads, states, attn_grams = attn_finish(
            mixed_arrived, out_arrived, moments[:4], self.owners
        )
        kept_attn, sent_attn = self.halves(attn_grams)
        received_attn = shift(sent_attn, "x", 1)
        main_factors = newton([jnp.concatenate([kept_down, kept_gate]), received_grams])
        turned_up, received_attn, received_last, main_factors, gains = lax.optimization_barrier(
            (turned_up, received_attn, received_last, main_factors, gains)
        )

        attn_arrived = self.arrive(self.send((kept_attn + received_attn)[:, None]))
        finished_up = finish(turned_up, self.z, moments[5], self.main)
        finished = finished_gate, finished_up, finished_down
        edges = jnp.zeros((self.owners, 3, HALF, HALF), jnp.float32)
        edges = lax.dynamic_update_slice_in_dim(
            edges, jnp.concatenate([v[2] for v in finished]), 0, 0
        )
        kept_rest, sent_rest = self.halves(edges)
        received_rest = shift(sent_rest, "x", 1)
        last_factor = newton([kept_last, received_last])
        main_line = self.along_sent(main_factors)
        gains = gains + shift(gains, "c", 1)
        attn_arrived, received_rest, last_factor, main_line, gains = lax.optimization_barrier(
            (attn_arrived, received_rest, last_factor, main_line, gains)
        )

        rest_arrived = self.arrive(self.send((kept_rest + received_rest)[:, None]))
        main_line = self.in_order(main_line)
        main_across = shift(main_line, "x", 1)
        factors = jnp.concatenate([last_factor, newton(attn_arrived)])
        gains = gains + shift(gains, "y", 1)
        rest_arrived, main_across, factors, gains = lax.optimization_barrier(
            (rest_arrived, main_across, factors, gains)
        )

        grads += [v[0] for v in finished]
        states += [v[1] for v in finished]
        line = self.along_sent(factors)
        rest_factors = newton(rest_arrived)
        gains = gains + shift(gains, "x", 1)
        line, rest_factors, gains = lax.optimization_barrier((line, rest_factors, gains))

        line = self.in_order(line)
        across = shift(line, "x", 1)
        rest_line = self.along_sent(rest_factors)
        main = self.main_blocks(main_line, main_across)
        across, rest_line = lax.optimization_barrier((across, rest_line))

        gains = gains + sum(shift(gains, "z", k) for k in range(1, self.depth))
        rest_line = self.in_order(rest_line)
        rest = self.both(rest_line, shift(rest_line, "x", 1))
        rest = rest.reshape((-1,) + rest.shape[3:])
        main = jnp.concatenate([main, self.main_blocks(line[:, :1], across[:, :1])])
        attn_factors = self.both(line[:, 1], across[:, 1])
        attn_factors = attn_factors.reshape((-1,) + attn_factors.shape[2:])
        counts, starts = spans(states[:4])
        updates = [apply_factor(v, attn_factors, s) for v, s in zip(states[:4], starts)]
        for i, order in enumerate((1, 2, 0)):
            blocks = main.shape[1]
            partly = apply_factor(states[4 + i], main[order], 0, 0, blocks)
            updates.append(apply_factor(states[4 + i], rest, i, blocks, blocks + 1, partly))
        return grads, states, updates, input_grad, gains

    def along_sent(self, values):
        return [values] + [shift(values, "z", k) for k in range(1, self.depth)]

    def in_order(self, arrived):
        line = jnp.zeros((self.depth,) + arrived[0].shape, arrived[0].dtype)
        for k, values in enumerate(arrived):
            line = place(line, values, self.back(k))
        return line

    def main_blocks(self, line, across):
        full = self.both(line, across)
        full = full.transpose(2, 1, 0, 3, 4, 5)
        return full.reshape(full.shape[:1] + (-1,) + full.shape[3:])

    def both(self, line, across):
        full = jnp.zeros((2,) + line.shape, line.dtype)
        return place(place(full, line, self.x), across, 1 - self.x)


def muon(ways, states):
    counts, starts = spans(states)
    slots = -(-sum(counts) // ways.owners) * ways.owners
    factors = ways.factor_gather(newton(ways.gram_sum(grams(states, slots))))
    return [apply_factor(state, factors, start) for state, start in zip(states, starts)]


def shards(
    ways,
    tokens,
    cotangent,
    dealt_lengths,
    norm_gains,
    query_weight,
    key_matrix,
    value_matrix,
    out_weight,
    gate_weight,
    up_weight,
    down_weight,
    moment_query,
    moment_key,
    moment_value,
    moment_out,
    moment_gate,
    moment_up,
    moment_down,
):
    ways.setup()
    local_rows = tokens.shape[0]
    segment, position, is_alive = slot_layout(dealt_lengths[0])
    rotary_cosines, rotary_sines = rope_tables(position)
    my_alive = lax.dynamic_slice_in_dim(is_alive, ways.part * local_rows, local_rows)
    query_cols = query_weight.shape[1]
    kv_cols = key_matrix.shape[1]
    kv_heads = kv_cols // HEAD_SIZE
    group_width = QUERY_HEADS // KEY_VALUE_HEADS
    cuts = (query_cols, query_cols + kv_cols)

    norm_gains = ways.features_in(norm_gains)
    inputs = ways.features_in(tokens).astype(jnp.float32)
    normalized_input, inverse_in = norm_forward(inputs, norm_gains[0])
    normed_full, mixed_full, out_full, gate_full = ways.open(
        normalized_input.astype(jnp.bfloat16),
        (query_weight, key_matrix, value_matrix),
        out_weight,
        gate_weight,
        up_weight,
        down_weight,
        (moment_down, moment_gate, moment_up),
    )
    projected = jnp.dot(normed_full, mixed_full, preferred_element_type=jnp.float32)
    alive_flags = is_alive.astype(jnp.int32)
    marks = (segment[:, None], segment[None, :], alive_flags[:, None], alive_flags[None, :])
    heads = query_cols // HEAD_SIZE
    square = jax.ShapeDtypeStruct((heads, GROUP_SLOTS, GROUP_SLOTS), jnp.float32)
    narrow_rows = [
        jax.ShapeDtypeStruct((GROUP_SLOTS, c), jnp.bfloat16)
        for c in (query_cols, kv_cols, kv_cols, query_cols)
    ]
    *kept_attention, mixed_heads = whole_call(
        partial(attend_body, kv_heads, group_width),
        [*narrow_rows[:3], square, square, narrow_rows[3]],
        projected,
        rotary_cosines,
        rotary_sines,
        *marks,
    )
    partial_attended, up_full = ways.beside_attention(contract_last(mixed_heads, out_full))
    attended = ways.beside_sum(partial_attended)
    normed_attn, inverse_attn = norm_forward(attended, norm_gains[1])
    middle = inputs + normed_attn
    normed_mid, inverse_mid = norm_forward(middle, norm_gains[2])
    mid_full = ways.beside_rows(normed_mid.astype(jnp.bfloat16))
    hidden, activated, pulled = enter(mid_full, gate_full, up_full)
    hidden, down_full = ways.beside_hidden(hidden)
    feed_out, _ = ways.mlp_sum([hidden], [down_full])
    normed_feed, inverse_feed = norm_forward(feed_out, norm_gains[3])
    block_output = (middle + normed_feed).astype(jnp.bfloat16)

    upstream = jnp.where(my_alive[:, None], ways.features_in(cotangent).astype(jnp.float32), 0.0)
    delta_feed, gain_feed = norm_backward(feed_out, inverse_feed, norm_gains[3], upstream)
    feed_grad = ways.mlp_rows(delta_feed.astype(jnp.bfloat16))
    partial_down = outer(feed_grad, hidden)
    total_down = ways.mlp_sum_rows(partial_down)
    feed_grad = after(feed_grad, partial_down)
    delta_gate, delta_up = leave(feed_grad, down_full, activated, pulled)
    delta_mid, token = ways.mlp_sum([delta_gate, delta_up], [gate_full, up_full])
    total_gate = ways.mlp_sum_rows(outer(after(mid_full, token), delta_gate))

    mid_back, gain_mid = norm_backward(middle, inverse_mid, norm_gains[2], delta_mid)
    delta_middle = upstream + mid_back
    delta_attended, gain_attn = norm_backward(attended, inverse_attn, norm_gains[1], delta_middle)
    attn_grad = ways.attn_rows_beside(delta_attended.astype(jnp.bfloat16))
    total_up = ways.mlp_sum_rows(outer(after(mid_full, attn_grad), delta_up))
    partial_out = narrow(contract_first(attn_grad, mixed_heads))

    def attention_backward(start):
        delta_mixed = narrow(product(after(attn_grad, start), out_full))
        delta_mixed_proj = whole_call(
            partial(attend_back_body, kv_heads, group_width),
            jax.ShapeDtypeStruct((GROUP_SLOTS, query_cols + 2 * kv_cols), jnp.bfloat16),
            delta_mixed,
            rotary_cosines,
            rotary_sines,
            *marks,
            *kept_attention,
        )
        partial_mixed = narrow(contract_first(normed_full, delta_mixed_proj))
        return partial_mixed, contract_last(delta_mixed_proj, mixed_full)

    moments = (
        moment_query,
        moment_key,
        moment_value,
        moment_out,
        moment_gate,
        moment_up,
        moment_down,
    )
    def end_norm(delta_normed):
        in_back, gain_in = norm_backward(inputs, inverse_in, norm_gains[0], delta_normed)
        gains = jnp.stack([gain_in, gain_attn, gain_mid, gain_feed])
        return delta_middle + in_back, gains

    grads, states, updates, input_grad, gain_grads = ways.close(
        partial_out, attention_backward, (total_down, total_gate, total_up), moments, end_norm
    )
    return (
        ways.features_out(block_output),
        ways.features_out(input_grad),
        ways.features_out(gain_grads),
        *grads,
        *states,
        *updates,
    )


def solution(mesh):
    sizes = dict(mesh.shape)
    if sizes == {"dp": 8, "tensor": 4}:
        mesh = Mesh(mesh.devices.reshape(4, 2, 2, 2), ("z", "x", "y", "c"))
        ways = Grid(dict(mesh.shape))
    else:
        ways = Plain(sizes)
    token_spec, weight_spec = ways.token_spec, ways.weight_spec
    return jax.shard_map(
        partial(shards, ways),
        mesh=mesh,
        in_specs=(token_spec, token_spec, ways.length_spec, P()) + (weight_spec,) * 14,
        out_specs=(token_spec, token_spec, P()) + (weight_spec,) * 21,
        check_vma=False,
    )
```
